256 devices in a mesh: dp: 4 (over x), vocab: 64 (over z, y, core).
Axes of the slice: x: 4, y: 4, z: 8, core: 2. Of those that a mesh axis runs over, the one named last changes fastest.
Arguments:
- hidden: bfloat16 [1024, 5120], P(('dp', 'vocab')), may hold values from -8 to 8
- teacher: bfloat16 [1024, 75968], P(('dp', 'vocab')), may hold values from -14 to 230
- head_weight: bfloat16 [5120, 75968], P('dp', 'vocab'), as said below
- loss_weight: float32 [1024], P(('dp', 'vocab')), may hold values from 1 to 10
Outputs:
- grad_hidden: bfloat16 [1024, 5120], P(('dp', 'vocab'))
- grad_head: bfloat16 [5120, 75968], P('dp', 'vocab')
The draws below stay inside these ranges and needn't reach their ends.
Inputs may be any that keep to these rules, and one draw needn't show every extreme that they name: `head_weight`: entries lie within plus or minus 12 / sqrt(5120).
All inputs are finite; a program needn't handle non-finite values.
Results may differ from the reference program's by a relative error of at most 0.024.
Values may be sent and summed in bfloat16 or wider, within the bound.
No kernel may reach another device: no remote copies, remote signals or barrier semaphores. Data moves between devices by JAX's collectives and lax.ppermute only.
A program may use at most 128 MiB of HBM per device.

```python
import math
import jax
import jax.numpy as jnp
from jax import lax

D = 5120
V = 75968
SPAN = 256
TOKENS = 1024


def head_columns(key, columns):
    base_key = jax.random.fold_in(key, 101)
    values = jax.vmap(lambda column: jax.random.normal(jax.random.fold_in(base_key, column), (D,), jnp.float32))(columns)
    return jnp.clip(values, -4.0, 4.0) * (3.0 / math.sqrt(D))


def draw_head_weight(key, part):
    return head_columns(key, jnp.arange(V)).T.astype(jnp.bfloat16)


def draw_hidden(key, part):
    own_key = jax.random.fold_in(key, 7)
    values = jax.random.normal(own_key, (TOKENS, D), jnp.float32)
    return jnp.clip(values, -8.0, 8.0).astype(jnp.bfloat16)


def draw_teacher(key, part):
    own_key = jax.random.fold_in(key, 11)
    return jnp.clip(3.0 * jax.random.normal(own_key, (TOKENS, V), jnp.float32), -14.0, 14.0).astype(jnp.bfloat16)


def shard_levels(rng, dims, cuts, smallest, largest):
    level, own = 1.0, jax.random.fold_in(rng, 6)
    for axis_at, parts in cuts:
        draws = jnp.exp(jax.random.uniform(jax.random.fold_in(own, axis_at), (parts,), jnp.float32, smallest / len(cuts), largest / len(cuts)))
        level = level * jnp.repeat(draws, dims[axis_at] // parts).reshape([-1 if axis == axis_at else 1 for axis in range(len(dims))])
    return level


def setup_inputs(seed: int = 0) -> dict:
    splits = jax.random.split(jax.random.key(seed), 5)
    hidden = draw_hidden(jax.random.fold_in(splits[4], 71), 0)
    teacher = draw_teacher(jax.random.fold_in(splits[4], 71), 0)
    head_weight = draw_head_weight(jax.random.fold_in(splits[4], 71), 0)
    loss_weight = jnp.clip(jnp.exp(math.log(10.0) - 2.3025851 * jax.random.uniform(splits[3], (TOKENS,), jnp.float32) ** shard_levels(splits[3], (TOKENS,), ((0, 256),), -0.2, 0.2)), 1.0, 10.0)
    return dict(hidden=hidden, teacher=teacher, head_weight=head_weight, loss_weight=loss_weight)


alpha_power = 0.5
beta_power = 0.25
joint_power = 0.75


def log_softmax_rows(values):
    top_value = jnp.max(values, axis=1, keepdims=True)
    return values - top_value - jnp.log(jnp.sum(jnp.exp(values - top_value), axis=1, keepdims=True))


def reference(hidden, teacher, head_weight, loss_weight):
    groups = TOKENS // SPAN
    hidden_groups = hidden.reshape(groups, SPAN, D)
    teacher_groups = teacher.reshape(groups, SPAN, V)
    weight_groups = loss_weight.reshape(groups, SPAN)

    def step(carry, inputs):
        group_hidden, group_teacher, group_weight = inputs
        logits = jnp.dot(group_hidden, head_weight, preferred_element_type=jnp.float32)
        log_student = log_softmax_rows(logits)
        log_teacher = log_softmax_rows(group_teacher.astype(jnp.float32))
        mixed = jnp.exp(alpha_power * log_teacher + beta_power * log_student) - jnp.exp(joint_power * log_student)
        remainder = jnp.sum(mixed, axis=1, keepdims=True)
        grad_logits = (-(group_weight / alpha_power)[:, None] * (mixed - jnp.exp(log_student) * remainder)).astype(jnp.bfloat16)
        grad_rows = lax.dot_general(grad_logits, head_weight, (((1,), (1,)), ((), ())), preferred_element_type=jnp.float32)
        group_head = lax.dot_general(group_hidden, grad_logits, (((0,), (0,)), ((), ())), preferred_element_type=jnp.float32)
        group_head = lax.optimization_barrier(group_head.astype(jnp.bfloat16)).astype(jnp.float32)
        return carry + group_head, grad_rows.astype(jnp.bfloat16)

    start_sum = jnp.zeros((D, V), jnp.float32)
    head_sum, grad_rows = lax.scan(step, start_sum, (hidden_groups, teacher_groups, weight_groups))
    return grad_rows.reshape(TOKENS, D), head_sum.astype(jnp.bfloat16)
```

```python
import jax
import jax.numpy as jnp
from jax import lax
from jax.sharding import Mesh, PartitionSpec as P

alpha_power = 0.5
beta_power = 0.25
joint_power = 0.75
smallest = 1e-37

NX, NZ, NY, NC = 4, 8, 4, 2
VOCAB = ("z", "y", "c")
OWN = 4
COLS = 1280
SLICE = 1187
SPAN = 256


def shift(count, by):
    return [(i, (i + by) % count) for i in range(count)]


def take(value, index, axis):
    return lax.dynamic_index_in_dim(value, index, axis, keepdims=False)


def rolled(value, by):
    count = value.shape[0]
    return lax.dynamic_slice_in_dim(jnp.concatenate([value, value], axis=0), by, count, axis=0)


def gather_hidden(hidden, x, y, c):
    pieces = hidden.reshape(OWN, NX, COLS).transpose(1, 0, 2)
    spread = jnp.broadcast_to(pieces[:, None], (NX, NZ, OWN, COLS)).reshape(NX * NZ, OWN, COLS)
    got = lax.all_to_all(spread, ("x", "z"), 0, 0, tiled=True)
    mine = rolled(got.reshape(NX, NZ * OWN, COLS), x)
    half = jnp.zeros((NX, NY, NZ * OWN, COLS), mine.dtype)
    half = lax.dynamic_update_slice(half, mine[:, None], (0, y, 0, 0))
    for by in range(1, NY):
        part = lax.ppermute(mine, "y", shift(NY, by))
        half = lax.dynamic_update_slice(half, part[:, None], (0, (y - by) % NY, 0, 0))
    other = lax.ppermute(half, "c", shift(NC, 1))
    whole = jnp.zeros((NX, NC) + half.shape[1:], half.dtype)
    whole = lax.dynamic_update_slice(whole, half[:, None], (0, c, 0, 0, 0))
    whole = lax.dynamic_update_slice(whole, other[:, None], (0, 1 - c, 0, 0, 0))
    return whole.reshape(NX, SPAN, COLS)


def split_three(value):
    high = value.astype(jnp.bfloat16)
    rest = value - high.astype(jnp.float32)
    middle = rest.astype(jnp.bfloat16)
    low = (rest - middle.astype(jnp.float32)).astype(jnp.bfloat16)
    return jnp.stack([high, middle, low], axis=-1)


def gather_teacher(teacher, loss_weight):
    parts = teacher.reshape(OWN, NZ * NY * NC, SLICE)
    weights = jnp.broadcast_to(split_three(loss_weight)[:, None], (OWN, NZ * NY * NC, 3))
    rows = jnp.concatenate([parts, weights], axis=2).transpose(1, 0, 2)
    got = lax.all_to_all(rows, VOCAB, 0, 0, tiled=True)
    got = got.reshape(NZ, NY, NC, OWN, SLICE + 3).transpose(4, 2, 1, 0, 3).reshape(SLICE + 3, SPAN)
    got = got.astype(jnp.float32)
    return got[:SLICE], got[SLICE] + got[SLICE + 1] + got[SLICE + 2]


def row_stats(student, teacher):
    top_s = jnp.max(student, axis=0)
    top_t = jnp.max(teacher, axis=0)
    s = student - top_s
    t = teacher - top_t

    def log_sum(value):
        return jnp.log(jnp.maximum(jnp.sum(jnp.exp(value), axis=0), smallest))

    return jnp.stack(
        [
            top_s + log_sum(s),
            top_t + log_sum(t),
            alpha_power * top_t + beta_power * top_s + log_sum(alpha_power * t + beta_power * s),
            joint_power * top_s + log_sum(joint_power * s),
        ]
    )


def body(hidden, teacher, head_weight, loss_weight):
    x, y, c = lax.axis_index("x"), lax.axis_index("y"), lax.axis_index("c")
    head = head_weight.T
    rows = gather_hidden(hidden, x, y, c)
    teacher_slice, weight = gather_teacher(teacher, loss_weight)

    def partial_logits(which):
        return lax.dot_general(
            head, rows[which], (((1,), (1,)), ((), ())), preferred_element_type=jnp.float32
        )

    sent = [
        lax.ppermute(partial_logits(r).astype(jnp.float16), "x", shift(NX, r)) for r in (2, 1, 3)
    ]
    logits = partial_logits(0)
    for part in sent:
        logits = logits + part.astype(jnp.float32)

    own = row_stats(logits, teacher_slice).reshape(8, 128)
    every = lax.all_to_all(
        jnp.broadcast_to(own[None], (NZ * NY * NC, 8, 128)), VOCAB, 0, 0, tiled=True
    ).reshape(NZ * NY * NC, 4, SPAN)
    top = jnp.max(every, axis=0)
    log_s, log_t, log_m, log_j = top + jnp.log(jnp.sum(jnp.exp(every - top), axis=0))
    remainder = jnp.exp(log_m - alpha_power * log_t - beta_power * log_s) - jnp.exp(
        log_j - joint_power * log_s
    )
    log_student = logits - log_s
    log_teacher = teacher_slice - log_t
    grad_logits = (
        -(weight / alpha_power)
        * (
            jnp.exp(alpha_power * log_teacher + beta_power * log_student)
            - jnp.exp(joint_power * log_student)
            - jnp.exp(log_student) * remainder
        )
    ).astype(jnp.bfloat16)

    groups = [grad_logits] + [
        lax.ppermute(grad_logits, "x", shift(NX, -r)) for r in range(1, NX)
    ]
    grads = jnp.concatenate(groups, axis=1)
    hidden_partial = lax.dot_general(
        grads, head, (((0,), (0,)), ((), ())), preferred_element_type=jnp.float32
    ).reshape(NX, NC, NY, NZ * OWN, COLS)
    away = lax.ppermute(take(hidden_partial, 1 - c, 1).astype(jnp.bfloat16), "c", shift(NC, 1))
    kept = take(hidden_partial, c, 1) + away.astype(jnp.float32)
    mine = take(kept, y, 1)
    for by in range(1, NY):
        part = take(kept, (y + by) % NY, 1).astype(jnp.bfloat16)
        mine = mine + lax.ppermute(part, "y", shift(NY, by)).astype(jnp.float32)
    mine = rolled(mine.astype(jnp.bfloat16), (NX - x) % NX)
    got = lax.all_to_all(mine.reshape(NX * NZ, OWN, COLS), ("x", "z"), 0, 0, tiled=True)
    total = jnp.sum(got.reshape(NX, NZ, OWN, COLS).astype(jnp.float32), axis=1)
    grad_hidden = total.transpose(1, 0, 2).reshape(OWN, NX * COLS).astype(jnp.bfloat16)
    grad_head = lax.dot_general(
        grads,
        rows.reshape(NX * SPAN, COLS),
        (((1,), (0,)), ((), ())),
        preferred_element_type=jnp.float32,
    ).astype(jnp.bfloat16)
    return grad_hidden, grad_head.T


def solution(mesh):
    fine = Mesh(mesh.devices.reshape(NX, NZ, NY, NC), ("x", "z", "y", "c"))
    every = ("x", "z", "y", "c")
    placed = (P(every, None), P(every, None), P("x", VOCAB), P(every))
    return jax.shard_map(
        body,
        mesh=fine,
        in_specs=placed,
        out_specs=(P(every, None), P("x", VOCAB)),
        check_vma=False,
    )
```

```python
import jax
import jax.numpy as jnp
from jax import lax
from jax.sharding import Mesh, PartitionSpec as P

alpha_power = 0.5
beta_power = 0.25
joint_power = 0.75
smallest = 1e-37

NX, NZ, NY, NC = 4, 8, 4, 2
VOCAB = ("z", "y", "c")
OWN = 4
COLS = 1280
SLICE = 1187
SPAN = 256


def shift(count, by):
    return [(i, (i + by) % count) for i in range(count)]


def rolled(value, by):
    count = value.shape[0]
    return lax.dynamic_slice_in_dim(jnp.concatenate([value, value], axis=0), by, count, axis=0)


def gather_hidden(hidden, x):
    pieces = hidden.reshape(OWN, NX, COLS).transpose(1, 0, 2)
    spread = jnp.broadcast_to(pieces[:, None], (NX, NZ, OWN, COLS)).reshape(NX * NZ, OWN, COLS)
    got = lax.all_to_all(spread, ("x", "z"), 0, 0, tiled=True)
    mine = rolled(got.reshape(NX, NZ * OWN, COLS), x)
    near = [mine] + [lax.ppermute(mine, "y", shift(NY, by)) for by in range(1, NY)]
    far = [lax.ppermute(block, "c", shift(NC, 1)) for block in near]
    return jnp.concatenate(near + far, axis=1)


def order(y, c):
    place = jnp.arange(SPAN)
    core, back, z, own = place // 128, place // 32 % NY, place // OWN % NZ, place % OWN
    true = ((z * NY + (y - back) % NY) * NC + (c + core) % NC) * OWN + own
    return place[:, None] == true[None, :]


def split_three(value):
    high = value.astype(jnp.bfloat16)
    rest = value - high.astype(jnp.float32)
    middle = rest.astype(jnp.bfloat16)
    low = (rest - middle.astype(jnp.float32)).astype(jnp.bfloat16)
    return jnp.stack([high, middle, low], axis=-1)


def teacher_rows(teacher, loss_weight):
    parts = teacher.reshape(OWN, NZ * NY * NC, SLICE)
    weights = jnp.broadcast_to(split_three(loss_weight)[:, None], (OWN, NZ * NY * NC, 3))
    return jnp.concatenate([parts, weights], axis=2).transpose(1, 0, 2)


def gather_teacher(rows, chosen):
    got = lax.all_to_all(rows, VOCAB, 0, 0, tiled=True).reshape(SPAN, SLICE + 3)
    got = lax.dot_general(
        got,
        chosen.astype(jnp.bfloat16),
        (((0,), (0,)), ((), ())),
        preferred_element_type=jnp.float32,
    )
    return got[:SLICE], got[SLICE] + got[SLICE + 1] + got[SLICE + 2]


def row_stats(student, teacher):
    top_s = jnp.max(student, axis=0)
    top_t = jnp.max(teacher, axis=0)
    s = student - top_s
    t = teacher - top_t

    def log_sum(value):
        return jnp.log(jnp.maximum(jnp.sum(jnp.exp(value), axis=0), smallest))

    return jnp.stack(
        [
            top_s + log_sum(s),
            top_t + log_sum(t),
            alpha_power * top_t + beta_power * top_s + log_sum(alpha_power * t + beta_power * s),
            joint_power * top_s + log_sum(joint_power * s),
        ]
    )


def moved(value, chosen, axis):
    return lax.dot_general(
        value,
        chosen.astype(jnp.float32),
        (((1,), (axis,)), ((), ())),
        precision=lax.Precision.HIGHEST,
        preferred_element_type=jnp.float32,
    )


def body(hidden, teacher, head_weight, loss_weight):
    x, y, c = lax.axis_index("x"), lax.axis_index("y"), lax.axis_index("c")
    head = head_weight.T
    chosen = order(y, c)
    rows = gather_hidden(hidden, x)
    taught = teacher_rows(teacher, loss_weight)

    def partial_logits(which):
        return lax.dot_general(
            head, rows[which], (((1,), (1,)), ((), ())), preferred_element_type=jnp.float32
        )

    halves = [partial_logits(r).astype(jnp.float16) for r in (2, 1, 3)]
    halves[0], taught = lax.optimization_barrier((halves[0], taught))
    sent = [lax.ppermute(half, "x", shift(NX, r)) for half, r in zip(halves, (2, 1, 3))]
    teacher_slice, weight = gather_teacher(taught, chosen)
    logits = partial_logits(0)
    for part in sent:
        logits = logits + part.astype(jnp.float32)

    own = moved(row_stats(logits, teacher_slice), chosen, 1).reshape(8, 128)
    every = lax.all_to_all(
        jnp.broadcast_to(own[None], (NZ * NY * NC, 8, 128)), VOCAB, 0, 0, tiled=True
    ).reshape(NZ * NY * NC, 4, SPAN)
    top = jnp.max(every, axis=0)
    merged = top + jnp.log(jnp.sum(jnp.exp(every - top), axis=0))
    log_s, log_t, log_m, log_j = moved(merged, chosen, 0)
    remainder = jnp.exp(log_m - alpha_power * log_t - beta_power * log_s) - jnp.exp(
        log_j - joint_power * log_s
    )
    log_student = logits - log_s
    log_teacher = teacher_slice - log_t
    grad_logits = (
        -(weight / alpha_power)
        * (
            jnp.exp(alpha_power * log_teacher + beta_power * log_student)
            - jnp.exp(joint_power * log_student)
            - jnp.exp(log_student) * remainder
        )
    ).astype(jnp.bfloat16)

    groups = [grad_logits] + [
        lax.ppermute(grad_logits, "x", shift(NX, -r)) for r in range(1, NX)
    ]

    def shared(which):
        part = jnp.stack(
            [
                lax.dot_general(
                    groups[r], head, (((0,), (0,)), ((), ())), preferred_element_type=jnp.float32
                )
                for r in which
            ]
        ).reshape(len(which), NC, NY, NZ * OWN, COLS)
        away = lax.ppermute(part[:, 1].astype(jnp.bfloat16), "c", shift(NC, 1))
        both = part[:, 0] + away.astype(jnp.float32)
        mine = both[:, 0]
        for by in range(1, NY):
            away = lax.ppermute(both[:, by].astype(jnp.bfloat16), "y", shift(NY, -by))
            mine = mine + away.astype(jnp.float32)
        return mine.astype(jnp.bfloat16)

    early, late = shared((0, 1)), shared((2, 3))
    mine = rolled(jnp.concatenate([early, late], axis=0), (NX - x) % NX)
    got = lax.all_to_all(mine.reshape(NX * NZ, OWN, COLS), ("x", "z"), 0, 0, tiled=True)
    total = jnp.sum(got.reshape(NX, NZ, OWN, COLS).astype(jnp.float32), axis=1)
    grad_hidden = total.transpose(1, 0, 2).reshape(OWN, NX * COLS).astype(jnp.bfloat16)
    grad_head = lax.dot_general(
        jnp.concatenate(groups, axis=1),
        rows.reshape(NX * SPAN, COLS),
        (((1,), (0,)), ((), ())),
        preferred_element_type=jnp.float32,
    ).astype(jnp.bfloat16)
    return grad_hidden, grad_head.T


def solution(mesh):
    fine = Mesh(mesh.devices.reshape(NX, NZ, NY, NC), ("x", "z", "y", "c"))
    every = ("x", "z", "y", "c")
    placed = (P(every, None), P(every, None), P("x", VOCAB), P(every))
    return jax.shard_map(
        body,
        mesh=fine,
        in_specs=placed,
        out_specs=(P(every, None), P("x", VOCAB)),
        check_vma=False,
    )
```

```python
import jax
import jax.numpy as jnp
from jax import lax
from jax.experimental import pallas as pl
from jax.experimental.pallas import tpu as pltpu
from jax.sharding import Mesh, PartitionSpec as P

alpha_power = 0.5
beta_power = 0.25
joint_power = 0.75
smallest = 1e-37
far_below = -1e30

NX, NZ, NY, NC = 4, 8, 4, 2
VOCAB = ("z", "y", "c")
OWN = 4
COLS = 1280
SLICE = 1187
PADDED = 1200
TILE = 240
CHUNK = 80
SPAN = 256
HALF = 128


def shift(count, by):
    return [(i, (i + by) % count) for i in range(count)]


def rolled(value, by):
    count = value.shape[0]
    return lax.dynamic_slice_in_dim(jnp.concatenate([value, value], axis=0), by, count, axis=0)


def gather_hidden(hidden, x, taught):
    pieces = hidden.reshape(OWN, NX, COLS).transpose(1, 0, 2)
    spread = jnp.broadcast_to(pieces[:, None], (NX, NZ, OWN, COLS)).reshape(NX * NZ, OWN, COLS)
    got = lax.all_to_all(spread, ("x", "z"), 0, 0, tiled=True)
    mine = rolled(got.reshape(NX, NZ * OWN, COLS), x)
    mine, taught = lax.optimization_barrier((mine, taught))
    near = [mine] + [lax.ppermute(mine, "y", shift(NY, by)) for by in range(1, NY)]
    far = [lax.ppermute(block, "c", shift(NC, 1)) for block in near]
    return near + far, taught


def order(y, c):
    place = jnp.arange(SPAN)
    core, back, z, own = place // 128, place // 32 % NY, place // OWN % NZ, place % OWN
    true = ((z * NY + (y - back) % NY) * NC + (c + core) % NC) * OWN + own
    return place[:, None] == true[None, :]


def split_three(value):
    high = value.astype(jnp.bfloat16)
    rest = value - high.astype(jnp.float32)
    middle = rest.astype(jnp.bfloat16)
    low = (rest - middle.astype(jnp.float32)).astype(jnp.bfloat16)
    return jnp.stack([high, middle, low], axis=-1)


def teacher_rows(teacher, loss_weight):
    parts = teacher.reshape(OWN, NZ * NY * NC, SLICE)
    weights = jnp.pad(split_three(loss_weight), ((0, 0), (0, PADDED - SLICE - 3)))
    weights = jnp.broadcast_to(weights[:, None], (OWN, NZ * NY * NC, PADDED - SLICE))
    return jnp.concatenate([parts, weights], axis=2).transpose(1, 0, 2)


def gather_teacher(rows, chosen):
    got = lax.all_to_all(rows, VOCAB, 0, 0, tiled=True).reshape(SPAN, PADDED)
    return lax.dot_general(
        got,
        chosen.astype(jnp.bfloat16),
        (((0,), (0,)), ((), ())),
        preferred_element_type=jnp.float32,
    )


def code(value):
    square = value * value
    fourth = square * square
    return (fourth * fourth * value).astype(jnp.bfloat16)


def decode(coded):
    value = coded.astype(jnp.float32)
    size = jnp.abs(value)
    root = jnp.where(size > 1e-36, jnp.exp(jnp.log(jnp.maximum(size, 1e-36)) * (1.0 / 9.0)), 0.0)
    return jnp.where(value < 0.0, -root, root)


def times(left, right):
    return lax.dot_general(
        left, right, (((1,), (1,)), ((), ())), preferred_element_type=jnp.float32
    )


def call(kernel, grid, ins, outs, scratch, flops, moved, *args):
    return pl.pallas_call(
        kernel,
        grid=grid,
        in_specs=ins,
        out_specs=[spec for spec, _ in outs],
        out_shape=[jax.ShapeDtypeStruct(shape, dtype) for _, (shape, dtype) in outs],
        scratch_shapes=scratch,
        cost_estimate=pl.CostEstimate(flops=flops, bytes_accessed=moved, transcendentals=0),
        compiler_params=pltpu.CompilerParams(vmem_limit_bytes=40 * 2**20),
    )(*args)


def whole(*shape):
    return pl.BlockSpec(shape, lambda *_: (0,) * len(shape))


def tiled(width):
    return pl.BlockSpec((TILE, width), lambda i: (i, 0))


BLOCK = (NX, NZ * OWN, COLS)
PIECE = ((PADDED, HALF), jnp.bfloat16)
KEPT = ((PADDED, HALF), jnp.float32)


def relayed_partials(head, blocks):
    def kernel(head_ref, *refs):
        refs, (near_ref, far_ref, rows_ref) = refs[:8], refs[8:]

        @pl.when(pl.program_id(0) == 0)
        def _():
            for at, ref in enumerate(refs):
                rows_ref[32 * at : 32 * at + 32] = ref[0]

        got = times(head_ref[...], rows_ref[...])
        near_ref[...] = code(got[:, :HALF])
        far_ref[...] = code(got[:, HALF:])

    return call(
        kernel,
        (PADDED // TILE,),
        [tiled(COLS)] + [pl.BlockSpec((1, NZ * OWN, COLS), lambda i: (2, 0, 0))] * 8,
        [(tiled(HALF), PIECE), (tiled(HALF), PIECE)],
        [pltpu.VMEM((SPAN, COLS), jnp.bfloat16)],
        2 * PADDED * SPAN * COLS,
        4 * 10**6,
        head,
        *blocks,
    )


def other_partials(head, blocks):
    def kernel(head_ref, *refs):
        refs, (rows_ref, near3_ref, far1_ref, near1_ref, far3_ref, own_ref) = refs[:8], refs[8:]

        @pl.when(pl.program_id(0) == 0)
        def _():
            for at, ref in enumerate(refs):
                rows_ref[:, 32 * at : 32 * at + 32] = ref[...]

        left = head_ref[...]
        got = times(left, rows_ref[3])
        near3_ref[...] = code(got[:, :HALF])
        far3_ref[...] = got[:, HALF:]
        got = times(left, rows_ref[1])
        near1_ref[...] = got[:, :HALF]
        far1_ref[...] = code(got[:, HALF:])
        own_ref[...] = times(left, rows_ref[0])

    return call(
        kernel,
        (PADDED // TILE,),
        [tiled(COLS)] + [whole(*BLOCK)] * 8,
        [(whole(NX, SPAN, COLS), ((NX, SPAN, COLS), jnp.bfloat16))]
        + [(tiled(HALF), PIECE)] * 2
        + [(tiled(HALF), KEPT)] * 2
        + [(tiled(SPAN), ((PADDED, SPAN), jnp.float32))],
        [],
        6 * PADDED * SPAN * COLS,
        12 * 10**6,
        head,
        *blocks,
    )


def added(kept, arrived):
    def kernel(*refs):
        for ours, theirs, out in zip(refs[:2], refs[2:4], refs[4:]):
            out[...] = code(ours[...] + decode(theirs[...]))

    return call(
        kernel,
        (PADDED // TILE,),
        [tiled(HALF)] * 4,
        [(tiled(HALF), PIECE)] * 2,
        [],
        40 * PADDED * SPAN,
        2 * 10**6,
        *kept,
        *arrived,
    )


def chunks(step, start):
    return lax.fori_loop(
        0, PADDED // CHUNK, lambda i, carry: step(pl.ds(pl.multiple_of(i * CHUNK, CHUNK), CHUNK), i, carry), start
    )


def valid(i):
    return lax.broadcasted_iota(jnp.int32, (CHUNK, SPAN), 0) + i * CHUNK < SLICE


def folded(value, join):
    return join(value.reshape(CHUNK // 8, 8, SPAN), axis=0)


def exact(left, right, dims):
    return lax.dot_general(
        left, right, (dims, ((), ())), precision=lax.Precision.HIGHEST, preferred_element_type=jnp.float32
    )


def statistics(own, parts, teacher, chosen):
    def kernel(own_ref, a0, a1, b0, b1, teacher_ref, chosen_ref, logits_ref, sums_ref):
        def first(rows, i, tops):
            arrived = jnp.concatenate(
                [decode(a0[rows, :]) + decode(a1[rows, :]), decode(b0[rows, :]) + decode(b1[rows, :])],
                axis=1,
            )
            student = jnp.where(valid(i), own_ref[rows, :] + arrived, far_below)
            taught = jnp.where(valid(i), teacher_ref[rows, :], far_below)
            logits_ref[rows, :] = student
            return (
                jnp.maximum(tops[0], folded(student, jnp.max)),
                jnp.maximum(tops[1], folded(taught, jnp.max)),
            )

        lowest = jnp.full((8, SPAN), far_below, jnp.float32)
        top_s, top_t = chunks(first, (lowest, lowest))
        top_s = jnp.max(top_s, axis=0, keepdims=True)
        top_t = jnp.max(top_t, axis=0, keepdims=True)

        def second(rows, i, sums):
            s = logits_ref[rows, :] - top_s
            t = jnp.where(valid(i), teacher_ref[rows, :] - top_t, far_below)
            terms = (s, t, alpha_power * t + beta_power * s, joint_power * s)
            return tuple(so_far + folded(jnp.exp(term), jnp.sum) for so_far, term in zip(sums, terms))

        sums = chunks(second, (jnp.zeros((8, SPAN), jnp.float32),) * 4)
        tops = (top_s, top_t, alpha_power * top_t + beta_power * top_s, joint_power * top_s)
        rows = [
            top + jnp.log(jnp.maximum(jnp.sum(total, axis=0, keepdims=True), smallest))
            for top, total in zip(tops, sums)
        ]
        rows = exact(jnp.concatenate(rows + rows, axis=0), chosen_ref[...], ((1,), (1,)))
        packed = jnp.concatenate([rows[:4, :HALF], rows[:4, HALF:]], axis=0)
        sums_ref[...] = jnp.broadcast_to(packed[None], sums_ref.shape)

    logits = ((PADDED, SPAN), jnp.float32)
    sums = ((NZ * NY * NC, 8, HALF), jnp.float32)
    return call(
        kernel,
        (1,),
        [whole(PADDED, SPAN)] + [whole(PADDED, HALF)] * 4 + [whole(PADDED, SPAN), whole(SPAN, SPAN)],
        [(whole(*logits[0]), logits), (whole(*sums[0]), sums)],
        [],
        100 * PADDED * SPAN,
        5 * 10**6,
        own,
        *parts,
        teacher,
        chosen,
    )


def gradients(every, logits, teacher, chosen):
    def kernel(every_ref, logits_ref, teacher_ref, chosen_ref, near_ref, far_ref):
        sums = every_ref[...]
        top = jnp.max(sums, axis=0)
        merged = top + jnp.log(jnp.sum(jnp.exp(sums - top[None]), axis=0))
        merged = jnp.concatenate([merged[:4], merged[4:]], axis=1)
        merged = exact(jnp.concatenate([merged, merged], axis=0), chosen_ref[...], ((1,), (0,)))
        log_s, log_t, log_m, log_j = (merged[k : k + 1] for k in range(4))
        remainder = jnp.exp(log_m - alpha_power * log_t - beta_power * log_s) - jnp.exp(
            log_j - joint_power * log_s
        )
        tail = teacher_ref[SLICE - 3 : SLICE + 5, :]
        weight = -(tail[3:4] + tail[4:5] + tail[5:6]) / alpha_power

        def step(rows, i, carry):
            s = logits_ref[rows, :] - log_s
            t = jnp.where(valid(i), teacher_ref[rows, :] - log_t, far_below)
            got = (
                jnp.exp(alpha_power * t + beta_power * s)
                - jnp.exp(joint_power * s)
                - jnp.exp(s) * remainder
            )
            got = (weight * got).astype(jnp.bfloat16)
            near_ref[rows, :] = got[:, :HALF]
            far_ref[rows, :] = got[:, HALF:]
            return carry

        chunks(step, 0)

    return call(
        kernel,
        (1,),
        [whole(NZ * NY * NC, 8, HALF)] + [whole(PADDED, SPAN)] * 2 + [whole(SPAN, SPAN)],
        [(whole(PADDED, HALF), PIECE)] * 2,
        [],
        60 * PADDED * SPAN,
        4 * 10**6,
        every,
        logits,
        teacher,
        chosen,
    )


def head_gradient(pieces, rows):
    def kernel(*refs):
        left = jnp.concatenate([ref[...] for ref in refs[:8]], axis=1)
        refs[9][...] = jnp.dot(left, refs[8][...], preferred_element_type=jnp.float32).astype(
            jnp.bfloat16
        )

    return call(
        kernel,
        (PADDED // TILE,),
        [tiled(HALF)] * 8 + [whole(NX * SPAN, COLS)],
        [(tiled(COLS), ((SLICE, COLS), jnp.bfloat16))],
        [],
        2 * PADDED * COLS * NX * SPAN,
        9 * 10**6,
        *pieces,
        rows,
    )[0]


def body(hidden, teacher, head_weight, loss_weight):
    x, y, c = lax.axis_index("x"), lax.axis_index("y"), lax.axis_index("c")
    head = jnp.pad(head_weight.T, ((0, PADDED - SLICE), (0, 0)))
    chosen = order(y, c).astype(jnp.float32)
    blocks, taught = gather_hidden(hidden, x, teacher_rows(teacher, loss_weight))

    def sent(value, by):
        return lax.ppermute(value, "x", shift(NX, by))

    relay = relayed_partials(head, blocks)
    relay = [sent(relay[0], 1), sent(relay[1], -1)]
    rows, near3, far1, near1, far3, own = other_partials(head, blocks)
    direct = [sent(near3, -1), sent(far1, 1)]
    summed = added((near1, far3), relay)
    summed = [sent(summed[0], 1), sent(summed[1], -1)]
    taught = gather_teacher(taught, chosen)
    logits, sums = statistics(own, (direct[0], summed[0], direct[1], summed[1]), taught, chosen)
    every = lax.all_to_all(sums, VOCAB, 0, 0, tiled=True)
    near, far = gradients(every, logits, taught, chosen)

    def passed(value, by):
        return lax.ppermute(value, "x", shift(NX, by))

    near = [near, passed(near, -1), None, passed(near, 1)]
    far = [far, passed(far, -1), None, passed(far, 1)]
    near[2], far[2] = passed(near[1], -1), passed(far[3], 1)

    def rows_of(parts, which):
        return jnp.stack(
            [
                lax.dot_general(
                    parts[r], head, (((0,), (0,)), ((), ())), preferred_element_type=jnp.float32
                )
                for r in which
            ]
        ).reshape(len(which), NY, NZ * OWN, COLS)

    def across(which):
        away = lax.ppermute(rows_of(far, which).astype(jnp.bfloat16), "c", shift(NC, 1))
        both = rows_of(near, which) + away.astype(jnp.float32)
        return both[:, 0], [both[:, by].astype(jnp.bfloat16) for by in range(1, NY)]

    def along(others):
        return [lax.ppermute(part, "y", shift(NY, -by)) for by, part in enumerate(others, 1)]

    def shared(mine, others):
        return (mine + sum(part.astype(jnp.float32) for part in others)).astype(jnp.bfloat16)

    mine, others = across((0, 1, 3))
    others = along(others)
    others[0], near[2], far[2] = lax.optimization_barrier((others[0], near[2], far[2]))
    late, far_others = across((2,))
    early, late = shared(mine, others), shared(late, along(far_others))
    early = jnp.concatenate([early[:2], late, early[2:]], axis=0)
    mine = rolled(early, (NX - x) % NX)
    got = lax.all_to_all(mine.reshape(NX * NZ, OWN, COLS), ("x", "z"), 0, 0, tiled=True)
    total = jnp.sum(got.reshape(NX, NZ, OWN, COLS).astype(jnp.float32), axis=1)
    grad_hidden = total.transpose(1, 0, 2).reshape(OWN, NX * COLS).astype(jnp.bfloat16)
    pieces = [part for pair in zip(near, far) for part in pair]
    grad_head = head_gradient(pieces, rows.reshape(NX * SPAN, COLS))
    return grad_hidden, grad_head.T


def solution(mesh):
    fine = Mesh(mesh.devices.reshape(NX, NZ, NY, NC), ("x", "z", "y", "c"))
    every = ("x", "z", "y", "c")
    placed = (P(every, None), P(every, None), P("x", VOCAB), P(every))
    return jax.shard_map(
        body,
        mesh=fine,
        in_specs=placed,
        out_specs=(P(every, None), P("x", VOCAB)),
        check_vma=False,
    )
```

```python
import jax
import jax.numpy as jnp
from jax import lax
from jax.experimental import pallas as pl
from jax.experimental.pallas import tpu as pltpu
from jax.sharding import Mesh, PartitionSpec as P

alpha_power = 0.5
beta_power = 0.25
joint_power = 0.75
smallest = 1e-37
far_below = -1e30

NX, NZ, NY, NC = 4, 8, 4, 2
VOCAB = ("z", "y", "c")
OWN = 4
COLS = 1280
SLICE = 1187
PADDED = 1200
TILE = 240
CHUNK = 240
LONG = 600
SPAN = 256
HALF = 128


def shift(count, by):
    return [(i, (i + by) % count) for i in range(count)]


def rolled(value, by):
    count = value.shape[0]
    return lax.dynamic_slice_in_dim(jnp.concatenate([value, value], axis=0), by, count, axis=0)


def gather_hidden(hidden, x, *ready):
    pieces = hidden.reshape(OWN, NX, COLS).transpose(1, 0, 2)
    spread = jnp.broadcast_to(pieces[:, None], (NX, NZ, OWN, COLS)).reshape(NX * NZ, OWN, COLS)
    got = lax.all_to_all(spread, ("x", "z"), 0, 0, tiled=True)
    mine = rolled(got.reshape(NX, NZ * OWN, COLS), x)
    mine, *ready = lax.optimization_barrier((mine, *ready))
    near = [mine] + [lax.ppermute(mine, "y", shift(NY, by)) for by in range(1, NY)]
    far = [lax.ppermute(block, "c", shift(NC, 1)) for block in near]
    return near + far, *ready


def order(y, c):
    place = jnp.arange(SPAN)
    core, back, z, own = place // 128, place // 32 % NY, place // OWN % NZ, place % OWN
    true = ((z * NY + (y - back) % NY) * NC + (c + core) % NC) * OWN + own
    return place[:, None] == true[None, :]


def split_three(value):
    high = value.astype(jnp.bfloat16)
    rest = value - high.astype(jnp.float32)
    middle = rest.astype(jnp.bfloat16)
    low = (rest - middle.astype(jnp.float32)).astype(jnp.bfloat16)
    return jnp.stack([high, middle, low], axis=-1)


def teacher_rows(teacher, loss_weight):
    parts = teacher.reshape(OWN, NZ * NY * NC, SLICE)
    weights = jnp.pad(split_three(loss_weight), ((0, 0), (0, PADDED - SLICE - 3)))
    weights = jnp.broadcast_to(weights[:, None], (OWN, NZ * NY * NC, PADDED - SLICE))
    return jnp.concatenate([parts, weights], axis=2).transpose(1, 0, 2)


def gather_teacher(rows, chosen):
    got = lax.all_to_all(rows, VOCAB, 0, 0, tiled=True).reshape(SPAN, PADDED)
    return lax.dot_general(
        got,
        chosen.astype(jnp.bfloat16),
        (((0,), (0,)), ((), ())),
        preferred_element_type=jnp.float32,
    )


def code(value):
    square = value * value
    fourth = square * square
    return (fourth * fourth * value).astype(jnp.bfloat16)


def decode(coded):
    value = coded.astype(jnp.float32)
    size = jnp.abs(value)
    root = jnp.exp2(jnp.log2(jnp.maximum(size, 1e-37)) * (1.0 / 9.0))
    return jnp.where(value < 0.0, -root, jnp.where(value > 0.0, root, 0.0))


def times(left, right):
    return lax.dot_general(
        left, right, (((1,), (1,)), ((), ())), preferred_element_type=jnp.float32
    )


def local(kernel, outs, scratch, flops, *args):
    place = pl.BlockSpec(memory_space=pltpu.VMEM)
    return pl.pallas_call(
        kernel,
        in_specs=[place] * len(args),
        out_specs=[place] * len(outs),
        out_shape=[jax.ShapeDtypeStruct(shape, dtype) for shape, dtype in outs],
        scratch_shapes=scratch,
        cost_estimate=pl.CostEstimate(flops=flops, bytes_accessed=10**6, transcendentals=0),
        compiler_params=pltpu.CompilerParams(vmem_limit_bytes=12 * 2**20),
    )(*args)


def whole(shape):
    return pl.BlockSpec(shape, lambda *_: (0,) * len(shape))


def streamed(kernel, outs, flops, *args):
    return pl.pallas_call(
        kernel,
        grid=(1,),
        in_specs=[whole(arg.shape) for arg in args],
        out_specs=[whole(shape) for shape, _ in outs],
        out_shape=[jax.ShapeDtypeStruct(shape, dtype) for shape, dtype in outs],
        cost_estimate=pl.CostEstimate(flops=flops, bytes_accessed=5 * 10**6, transcendentals=0),
        compiler_params=pltpu.CompilerParams(vmem_limit_bytes=40 * 2**20),
    )(*args)


PIECE = ((PADDED, HALF), jnp.bfloat16)
KEPT = ((PADDED, HALF), jnp.float32)


def chunks(size, step, start):
    def at(i, carry):
        return step(pl.ds(pl.multiple_of(i * size, size), size), i, carry)

    return lax.fori_loop(0, PADDED // size, at, start)


def relayed_partials(head, blocks):
    def kernel(head_ref, *refs):
        refs, (near_ref, far_ref, rows_ref) = refs[:8], refs[8:]
        for at, ref in enumerate(refs):
            rows_ref[32 * at : 32 * at + 32] = ref[2]

        got = times(head_ref[...], rows_ref[...])
        near_ref[...] = code(got[:, :HALF])
        far_ref[...] = code(got[:, HALF:])

    return local(
        kernel,
        [PIECE, PIECE],
        [pltpu.VMEM((SPAN, COLS), jnp.bfloat16)],
        2 * PADDED * SPAN * COLS,
        head,
        *blocks,
    )


def other_partials(head, blocks):
    def kernel(head_ref, *refs):
        refs, (out_ref, near3_ref, far1_ref, near1_ref, far3_ref, own_ref, rows_ref, done) = (
            refs[:8],
            refs[8:],
        )
        for at, ref in enumerate(refs):
            rows_ref[:, 32 * at : 32 * at + 32] = ref[...]
        copy = pltpu.make_async_copy(rows_ref, out_ref, done)
        copy.start()

        def step(rows, i, carry):
            left = head_ref[rows, :]
            got = times(left, rows_ref[3])
            near3_ref[rows, :] = code(got[:, :HALF])
            far3_ref[rows, :] = got[:, HALF:]
            got = times(left, rows_ref[1])
            near1_ref[rows, :] = got[:, :HALF]
            far1_ref[rows, :] = code(got[:, HALF:])
            own_ref[rows, :] = times(left, rows_ref[0])
            return carry

        chunks(LONG, step, 0)
        copy.wait()

    place = pl.BlockSpec(memory_space=pltpu.VMEM)
    every = ((NX, SPAN, COLS), jnp.bfloat16)
    outs = [every, PIECE, PIECE, KEPT, KEPT, ((PADDED, SPAN), jnp.float32)]
    return pl.pallas_call(
        kernel,
        in_specs=[place] * 9,
        out_specs=[pl.BlockSpec(memory_space=pl.ANY)] + [place] * 5,
        out_shape=[jax.ShapeDtypeStruct(shape, dtype) for shape, dtype in outs],
        scratch_shapes=[pltpu.VMEM(*every), pltpu.SemaphoreType.DMA],
        cost_estimate=pl.CostEstimate(
            flops=6 * PADDED * SPAN * COLS, bytes_accessed=4 * 10**6, transcendentals=0
        ),
        compiler_params=pltpu.CompilerParams(vmem_limit_bytes=16 * 2**20),
    )(head, *blocks)


def added(kept, arrived):
    def kernel(*refs):
        def step(rows, i, carry):
            for ours, theirs, out in zip(refs[:2], refs[2:4], refs[4:]):
                out[rows, :] = code(ours[rows, :] + decode(theirs[rows, :]))
            return carry

        chunks(CHUNK, step, 0)

    return local(kernel, [PIECE, PIECE], [], 40 * PADDED * SPAN, *kept, *arrived)


def valid(i):
    return lax.broadcasted_iota(jnp.int32, (CHUNK, SPAN), 0) + i * CHUNK < SLICE


def folded(value, join):
    return join(value.reshape(CHUNK // 8, 8, SPAN), axis=0)


def exact(left, right, dims):
    return lax.dot_general(
        left, right, (dims, ((), ())), precision=lax.Precision.HIGHEST, preferred_element_type=jnp.float32
    )


def statistics(own, parts, teacher, chosen):
    def kernel(own_ref, a0, a1, b0, b1, teacher_ref, chosen_ref, logits_ref, sums_ref):
        def first(rows, i, tops):
            arrived = jnp.concatenate(
                [decode(a0[rows, :]) + decode(a1[rows, :]), decode(b0[rows, :]) + decode(b1[rows, :])],
                axis=1,
            )
            student = jnp.where(valid(i), own_ref[rows, :] + arrived, far_below)
            taught = jnp.where(valid(i), teacher_ref[rows, :], far_below)
            logits_ref[rows, :] = student
            return (
                jnp.maximum(tops[0], folded(student, jnp.max)),
                jnp.maximum(tops[1], folded(taught, jnp.max)),
            )

        lowest = jnp.full((8, SPAN), far_below, jnp.float32)
        top_s, top_t = chunks(CHUNK, first, (lowest, lowest))
        top_s = jnp.max(top_s, axis=0, keepdims=True)
        top_t = jnp.max(top_t, axis=0, keepdims=True)

        def second(rows, i, sums):
            s = logits_ref[rows, :] - top_s
            t = jnp.where(valid(i), teacher_ref[rows, :] - top_t, far_below)
            terms = (s, t, alpha_power * t + beta_power * s, joint_power * s)
            return tuple(so_far + folded(jnp.exp(term), jnp.sum) for so_far, term in zip(sums, terms))

        sums = chunks(CHUNK, second, (jnp.zeros((8, SPAN), jnp.float32),) * 4)
        tops = (top_s, top_t, alpha_power * top_t + beta_power * top_s, joint_power * top_s)
        rows = [
            top + jnp.log(jnp.maximum(jnp.sum(total, axis=0, keepdims=True), smallest))
            for top, total in zip(tops, sums)
        ]
        rows = exact(jnp.concatenate(rows + rows, axis=0), chosen_ref[...], ((1,), (1,)))
        packed = jnp.concatenate([rows[:4, :HALF], rows[:4, HALF:]], axis=0)
        sums_ref[...] = jnp.broadcast_to(packed[None], sums_ref.shape)

    return streamed(
        kernel,
        [((PADDED, SPAN), jnp.float32), ((NZ * NY * NC, 8, HALF), jnp.float32)],
        100 * PADDED * SPAN,
        own,
        *parts,
        teacher,
        chosen,
    )


def gradients(every, logits, teacher, chosen):
    def kernel(every_ref, logits_ref, teacher_ref, chosen_ref, near_ref, far_ref):
        sums = every_ref[...]
        top = jnp.max(sums, axis=0)
        merged = top + jnp.log(jnp.sum(jnp.exp(sums - top[None]), axis=0))
        merged = jnp.concatenate([merged[:4], merged[4:]], axis=1)
        merged = exact(jnp.concatenate([merged, merged], axis=0), chosen_ref[...], ((1,), (0,)))
        log_s, log_t, log_m, log_j = (merged[k : k + 1] for k in range(4))
        remainder = jnp.exp(log_m - alpha_power * log_t - beta_power * log_s) - jnp.exp(
            log_j - joint_power * log_s
        )
        tail = teacher_ref[SLICE - 3 : SLICE + 5, :]
        weight = -(tail[3:4] + tail[4:5] + tail[5:6]) / alpha_power

        def step(rows, i, carry):
            s = logits_ref[rows, :] - log_s
            t = jnp.where(valid(i), teacher_ref[rows, :] - log_t, far_below)
            got = (
                jnp.exp(alpha_power * t + beta_power * s)
                - jnp.exp(joint_power * s)
                - jnp.exp(s) * remainder
            )
            got = (weight * got).astype(jnp.bfloat16)
            near_ref[rows, :] = got[:, :HALF]
            far_ref[rows, :] = got[:, HALF:]
            return carry

        chunks(CHUNK, step, 0)

    return streamed(
        kernel, [PIECE, PIECE], 60 * PADDED * SPAN, every, logits, teacher, chosen
    )


def head_gradient(pieces, rows):
    def kernel(*refs):
        left = jnp.concatenate([ref[...] for ref in refs[:8]], axis=1)
        refs[9][...] = jnp.dot(left, refs[8][...], preferred_element_type=jnp.float32).astype(
            jnp.bfloat16
        )

    def tiled(width):
        return pl.BlockSpec((TILE, width), lambda i: (i, 0))

    return pl.pallas_call(
        kernel,
        grid=(PADDED // TILE,),
        in_specs=[tiled(HALF)] * 8 + [pl.BlockSpec((NX * SPAN, COLS), lambda i: (0, 0))],
        out_specs=tiled(COLS),
        out_shape=jax.ShapeDtypeStruct((SLICE, COLS), jnp.bfloat16),
        cost_estimate=pl.CostEstimate(
            flops=2 * PADDED * COLS * NX * SPAN, bytes_accessed=9 * 10**6, transcendentals=0
        ),
        compiler_params=pltpu.CompilerParams(vmem_limit_bytes=20 * 2**20),
    )(*pieces, rows)


def body(hidden, teacher, head_weight, loss_weight):
    x, y, c = lax.axis_index("x"), lax.axis_index("y"), lax.axis_index("c")
    head = jnp.pad(head_weight.T, ((0, PADDED - SLICE), (0, 0)))
    chosen = order(y, c).astype(jnp.float32)
    back = lax.rem(NX - x, NX).astype(jnp.uint32)
    blocks, taught, head, back = gather_hidden(
        hidden, x, teacher_rows(teacher, loss_weight), head, back
    )

    def sent(value, by):
        return lax.ppermute(value, "x", shift(NX, by))

    relay = relayed_partials(head, blocks)
    relay = [sent(relay[0], 1), sent(relay[1], -1)]
    rows, near3, far1, near1, far3, own = other_partials(head, blocks)
    direct = [sent(near3, -1), sent(far1, 1)]
    summed = added((near1, far3), relay)
    summed = [sent(summed[0], 1), sent(summed[1], -1)]
    taught = gather_teacher(taught, chosen)
    logits, sums = statistics(own, (direct[0], summed[0], direct[1], summed[1]), taught, chosen)
    every = lax.all_to_all(sums, VOCAB, 0, 0, tiled=True)
    near, far = gradients(every, logits, taught, chosen)

    def passed(value, by):
        return lax.ppermute(value, "x", shift(NX, by))

    near = [near, passed(near, -1), None, passed(near, 1)]
    far = [far, passed(far, -1), None, passed(far, 1)]
    near[2], far[2] = passed(near[1], -1), passed(far[3], 1)

    def rows_of(parts, which):
        return jnp.stack(
            [
                lax.dot_general(
                    parts[r], head, (((0,), (0,)), ((), ())), preferred_element_type=jnp.float32
                )
                for r in which
            ]
        ).reshape(len(which), NY, NZ * OWN, COLS)

    def across(which):
        away = lax.ppermute(rows_of(far, which).astype(jnp.bfloat16), "c", shift(NC, 1))
        both = rows_of(near, which) + away.astype(jnp.float32)
        return both[:, 0], [both[:, by].astype(jnp.bfloat16) for by in range(1, NY)]

    def along(others):
        return [lax.ppermute(part, "y", shift(NY, -by)) for by, part in enumerate(others, 1)]

    def shared(mine, others):
        return (mine + sum(part.astype(jnp.float32) for part in others)).astype(jnp.bfloat16)

    first, others = across((0,))
    first_others = along(others)
    first, near[1], far[1] = lax.optimization_barrier((first, near[1], far[1]))
    first_others, near[2], far[2] = lax.optimization_barrier((first_others, near[2], far[2]))
    rest, others = across((1, 2, 3))
    rest = shared(rest, along(others))
    mine = jnp.concatenate([shared(first, first_others), rest], axis=0)
    mine = rolled(mine, back)
    got = lax.all_to_all(mine.reshape(NX * NZ, OWN, COLS), ("x", "z"), 0, 0, tiled=True)
    total = jnp.sum(got.reshape(NX, NZ, OWN, COLS).astype(jnp.float32), axis=1)
    grad_hidden = total.transpose(1, 0, 2).reshape(OWN, NX * COLS).astype(jnp.bfloat16)
    pieces = [part for pair in zip(near, far) for part in pair]
    grad_head = head_gradient(pieces, rows.reshape(NX * SPAN, COLS))
    return grad_hidden, grad_head.T


def solution(mesh):
    fine = Mesh(mesh.devices.reshape(NX, NZ, NY, NC), ("x", "z", "y", "c"))
    every = ("x", "z", "y", "c")
    placed = (P(every, None), P(every, None), P("x", VOCAB), P(every))
    return jax.shard_map(
        body,
        mesh=fine,
        in_specs=placed,
        out_specs=(P(every, None), P("x", VOCAB)),
        check_vma=False,
    )
```

```python
import jax
import jax.numpy as jnp
from jax import lax
from jax.experimental import pallas as pl
from jax.experimental.pallas import tpu as pltpu
from jax.sharding import Mesh, PartitionSpec as P

alpha_power = 0.5
beta_power = 0.25
joint_power = 0.75
smallest = 1e-37
far_below = -1e30

NX, NZ, NY, NC = 4, 8, 4, 2
VOCAB = ("z", "y", "c")
OWN = 4
COLS = 1280
SLICE = 1187
PADDED = 1200
TILE = 240
CHUNK = 240
LONG = 600
SPAN = 256
HALF = 128


def shift(count, by):
    return [(i, (i + by) % count) for i in range(count)]


def rolled(value, by):
    count = value.shape[0]
    return lax.dynamic_slice_in_dim(jnp.concatenate([value, value], axis=0), by, count, axis=0)


def gather_hidden(hidden, x, *ready):
    pieces = hidden.reshape(OWN, NX, COLS).transpose(1, 0, 2)
    spread = jnp.broadcast_to(pieces[:, None], (NX, NZ, OWN, COLS)).reshape(NX * NZ, OWN, COLS)
    got = lax.all_to_all(spread, ("x", "z"), 0, 0, tiled=True)
    mine = rolled(got.reshape(NX, NZ * OWN, COLS), x)
    mine, *ready = lax.optimization_barrier((mine, *ready))
    near = [mine] + [lax.ppermute(mine, "y", shift(NY, by)) for by in range(1, NY)]
    far = [lax.ppermute(block, "c", shift(NC, 1)) for block in near]
    return near + far, *ready


def order(y, c):
    place = jnp.arange(SPAN)
    core, back, z, own = place // 128, place // 32 % NY, place // OWN % NZ, place % OWN
    true = ((z * NY + (y - back) % NY) * NC + (c + core) % NC) * OWN + own
    return place[:, None] == true[None, :]


def split_three(value):
    high = value.astype(jnp.bfloat16)
    rest = value - high.astype(jnp.float32)
    middle = rest.astype(jnp.bfloat16)
    low = (rest - middle.astype(jnp.float32)).astype(jnp.bfloat16)
    return jnp.stack([high, middle, low], axis=-1)


def teacher_rows(teacher, loss_weight):
    parts = teacher.reshape(OWN, NZ * NY * NC, SLICE)
    weights = jnp.pad(split_three(loss_weight), ((0, 0), (0, PADDED - SLICE - 3)))
    weights = jnp.broadcast_to(weights[:, None], (OWN, NZ * NY * NC, PADDED - SLICE))
    return jnp.concatenate([parts, weights], axis=2).transpose(1, 0, 2)


def gather_teacher(rows, chosen):
    got = lax.all_to_all(rows, VOCAB, 0, 0, tiled=True).reshape(SPAN, PADDED)
    return lax.dot_general(
        got,
        chosen.astype(jnp.bfloat16),
        (((0,), (0,)), ((), ())),
        preferred_element_type=jnp.float32,
    )


def code(value):
    square = value * value
    fourth = square * square
    return (fourth * fourth * value).astype(jnp.bfloat16)


def decode(coded):
    value = coded.astype(jnp.float32)
    size = jnp.abs(value)
    root = jnp.exp2(jnp.log2(jnp.maximum(size, 1e-37)) * (1.0 / 9.0))
    return jnp.where(value < 0.0, -root, jnp.where(value > 0.0, root, 0.0))


def times(left, right):
    return lax.dot_general(
        left, right, (((1,), (1,)), ((), ())), preferred_element_type=jnp.float32
    )


def local(kernel, outs, scratch, flops, *args):
    place = pl.BlockSpec(memory_space=pltpu.VMEM)
    return pl.pallas_call(
        kernel,
        in_specs=[place] * len(args),
        out_specs=[place] * len(outs),
        out_shape=[jax.ShapeDtypeStruct(shape, dtype) for shape, dtype in outs],
        scratch_shapes=scratch,
        cost_estimate=pl.CostEstimate(flops=flops, bytes_accessed=10**6, transcendentals=0),
        compiler_params=pltpu.CompilerParams(vmem_limit_bytes=12 * 2**20),
    )(*args)


def whole(shape):
    return pl.BlockSpec(shape, lambda *_: (0,) * len(shape))


def streamed(kernel, outs, flops, *args):
    return pl.pallas_call(
        kernel,
        grid=(1,),
        in_specs=[whole(arg.shape) for arg in args],
        out_specs=[whole(shape) for shape, _ in outs],
        out_shape=[jax.ShapeDtypeStruct(shape, dtype) for shape, dtype in outs],
        cost_estimate=pl.CostEstimate(flops=flops, bytes_accessed=5 * 10**6, transcendentals=0),
        compiler_params=pltpu.CompilerParams(vmem_limit_bytes=40 * 2**20),
    )(*args)


PIECE = ((PADDED, HALF), jnp.bfloat16)
KEPT = ((PADDED, HALF), jnp.float32)


def chunks(size, step, start):
    def at(i, carry):
        return step(pl.ds(pl.multiple_of(i * size, size), size), i, carry)

    return lax.fori_loop(0, PADDED // size, at, start)


def relayed_partials(head, blocks):
    def kernel(head_ref, *refs):
        refs, (near_ref, far_ref, rows_ref) = refs[:8], refs[8:]
        for at, ref in enumerate(refs):
            rows_ref[32 * at : 32 * at + 32] = ref[2]

        got = times(head_ref[...], rows_ref[...])
        near_ref[...] = code(got[:, :HALF])
        far_ref[...] = code(got[:, HALF:])

    return local(
        kernel,
        [PIECE, PIECE],
        [pltpu.VMEM((SPAN, COLS), jnp.bfloat16)],
        2 * PADDED * SPAN * COLS,
        head,
        *blocks,
    )


def other_partials(head, blocks):
    def kernel(head_ref, *refs):
        refs, (out_ref, near3_ref, far1_ref, near1_ref, far3_ref, own_ref, rows_ref, done) = (
            refs[:8],
            refs[8:],
        )
        for at, ref in enumerate(refs):
            rows_ref[:, 32 * at : 32 * at + 32] = ref[...]
        copy = pltpu.make_async_copy(rows_ref, out_ref, done)
        copy.start()

        def step(rows, i, carry):
            left = head_ref[rows, :]
            got = times(left, rows_ref[3])
            near3_ref[rows, :] = code(got[:, :HALF])
            far3_ref[rows, :] = got[:, HALF:]
            got = times(left, rows_ref[1])
            near1_ref[rows, :] = got[:, :HALF]
            far1_ref[rows, :] = code(got[:, HALF:])
            own_ref[rows, :] = times(left, rows_ref[0])
            return carry

        chunks(LONG, step, 0)
        copy.wait()

    place = pl.BlockSpec(memory_space=pltpu.VMEM)
    every = ((NX, SPAN, COLS), jnp.bfloat16)
    outs = [every, PIECE, PIECE, KEPT, KEPT, ((PADDED, SPAN), jnp.float32)]
    return pl.pallas_call(
        kernel,
        in_specs=[place] * 9,
        out_specs=[pl.BlockSpec(memory_space=pl.ANY)] + [place] * 5,
        out_shape=[jax.ShapeDtypeStruct(shape, dtype) for shape, dtype in outs],
        scratch_shapes=[pltpu.VMEM(*every), pltpu.SemaphoreType.DMA],
        cost_estimate=pl.CostEstimate(
            flops=6 * PADDED * SPAN * COLS, bytes_accessed=4 * 10**6, transcendentals=0
        ),
        compiler_params=pltpu.CompilerParams(vmem_limit_bytes=16 * 2**20),
    )(head, *blocks)


def added(kept, arrived):
    def kernel(*refs):
        def step(rows, i, carry):
            for ours, theirs, out in zip(refs[:2], refs[2:4], refs[4:]):
                out[rows, :] = code(ours[rows, :] + decode(theirs[rows, :]))
            return carry

        chunks(CHUNK, step, 0)

    return local(kernel, [PIECE, PIECE], [], 40 * PADDED * SPAN, *kept, *arrived)


def valid(i):
    return lax.broadcasted_iota(jnp.int32, (CHUNK, SPAN), 0) + i * CHUNK < SLICE


def folded(value, join):
    return join(value.reshape(CHUNK // 8, 8, SPAN), axis=0)


def exact(left, right, dims):
    return lax.dot_general(
        left, right, (dims, ((), ())), precision=lax.Precision.HIGHEST, preferred_element_type=jnp.float32
    )


def statistics(own, parts, teacher, chosen):
    def kernel(own_ref, a0, a1, b0, b1, teacher_ref, chosen_ref, logits_ref, sums_ref):
        def first(rows, i, tops):
            arrived = jnp.concatenate(
                [decode(a0[rows, :]) + decode(a1[rows, :]), decode(b0[rows, :]) + decode(b1[rows, :])],
                axis=1,
            )
            student = jnp.where(valid(i), own_ref[rows, :] + arrived, far_below)
            taught = jnp.where(valid(i), teacher_ref[rows, :], far_below)
            logits_ref[rows, :] = student
            return (
                jnp.maximum(tops[0], folded(student, jnp.max)),
                jnp.maximum(tops[1], folded(taught, jnp.max)),
            )

        lowest = jnp.full((8, SPAN), far_below, jnp.float32)
        top_s, top_t = chunks(CHUNK, first, (lowest, lowest))
        top_s = jnp.max(top_s, axis=0, keepdims=True)
        top_t = jnp.max(top_t, axis=0, keepdims=True)

        def second(rows, i, sums):
            s = logits_ref[rows, :] - top_s
            t = jnp.where(valid(i), teacher_ref[rows, :] - top_t, far_below)
            terms = (s, t, alpha_power * t + beta_power * s, joint_power * s)
            return tuple(so_far + folded(jnp.exp(term), jnp.sum) for so_far, term in zip(sums, terms))

        sums = chunks(CHUNK, second, (jnp.zeros((8, SPAN), jnp.float32),) * 4)
        tops = (top_s, top_t, alpha_power * top_t + beta_power * top_s, joint_power * top_s)
        rows = [
            top + jnp.log(jnp.maximum(jnp.sum(total, axis=0, keepdims=True), smallest))
            for top, total in zip(tops, sums)
        ]
        rows = exact(jnp.concatenate(rows + rows, axis=0), chosen_ref[...], ((1,), (1,)))
        packed = jnp.concatenate([rows[:4, :HALF], rows[:4, HALF:]], axis=0)
        sums_ref[...] = jnp.broadcast_to(packed[None], sums_ref.shape)

    return streamed(
        kernel,
        [((PADDED, SPAN), jnp.float32), ((NZ * NY * NC, 8, HALF), jnp.float32)],
        100 * PADDED * SPAN,
        own,
        *parts,
        teacher,
        chosen,
    )


def gradients(every, logits, teacher, chosen):
    def kernel(every_ref, logits_ref, teacher_ref, chosen_ref, near_ref, far_ref):
        sums = every_ref[...]
        top = jnp.max(sums, axis=0)
        merged = top + jnp.log(jnp.sum(jnp.exp(sums - top[None]), axis=0))
        merged = jnp.concatenate([merged[:4], merged[4:]], axis=1)
        merged = exact(jnp.concatenate([merged, merged], axis=0), chosen_ref[...], ((1,), (0,)))
        log_s, log_t, log_m, log_j = (merged[k : k + 1] for k in range(4))
        remainder = jnp.exp(log_m - alpha_power * log_t - beta_power * log_s) - jnp.exp(
            log_j - joint_power * log_s
        )
        tail = teacher_ref[SLICE - 3 : SLICE + 5, :]
        weight = -(tail[3:4] + tail[4:5] + tail[5:6]) / alpha_power

        def step(rows, i, carry):
            s = logits_ref[rows, :] - log_s
            t = jnp.where(valid(i), teacher_ref[rows, :] - log_t, far_below)
            got = (
                jnp.exp(alpha_power * t + beta_power * s)
                - jnp.exp(joint_power * s)
                - jnp.exp(s) * remainder
            )
            got = (weight * got).astype(jnp.bfloat16)
            near_ref[rows, :] = got[:, :HALF]
            far_ref[rows, :] = got[:, HALF:]
            return carry

        chunks(CHUNK, step, 0)

    return streamed(
        kernel, [PIECE, PIECE], 60 * PADDED * SPAN, every, logits, teacher, chosen
    )


def head_gradient(pieces, rows):
    def kernel(*refs):
        left = jnp.concatenate([ref[...] for ref in refs[:8]], axis=1)
        refs[9][...] = jnp.dot(left, refs[8][...], preferred_element_type=jnp.float32).astype(
            jnp.bfloat16
        )

    def tiled(width):
        return pl.BlockSpec((TILE, width), lambda i: (i, 0))

    return pl.pallas_call(
        kernel,
        grid=(PADDED // TILE,),
        in_specs=[tiled(HALF)] * 8 + [pl.BlockSpec((NX * SPAN, COLS), lambda i: (0, 0))],
        out_specs=tiled(COLS),
        out_shape=jax.ShapeDtypeStruct((SLICE, COLS), jnp.bfloat16),
        cost_estimate=pl.CostEstimate(
            flops=2 * PADDED * COLS * NX * SPAN, bytes_accessed=9 * 10**6, transcendentals=0
        ),
        compiler_params=pltpu.CompilerParams(vmem_limit_bytes=20 * 2**20),
    )(*pieces, rows)


def body(hidden, teacher, head_weight, loss_weight):
    x, y, c = lax.axis_index("x"), lax.axis_index("y"), lax.axis_index("c")
    head = jnp.pad(head_weight.T, ((0, PADDED - SLICE), (0, 0)))
    chosen = order(y, c).astype(jnp.float32)
    back = lax.rem(NX - x, NX).astype(jnp.uint32)
    blocks, taught, head, back = gather_hidden(
        hidden, x, teacher_rows(teacher, loss_weight), head, back
    )

    def sent(value, by):
        return lax.ppermute(value, "x", shift(NX, by))

    relay = relayed_partials(head, blocks)
    relay = [sent(relay[0], 1), sent(relay[1], -1)]
    rows, near3, far1, near1, far3, own = other_partials(head, blocks)
    direct = [sent(near3, -1), sent(far1, 1)]
    summed = added((near1, far3), relay)
    summed = [sent(summed[0], 1), sent(summed[1], -1)]
    taught = gather_teacher(taught, chosen)
    logits, sums = statistics(own, (direct[0], summed[0], direct[1], summed[1]), taught, chosen)
    every = lax.all_to_all(sums, VOCAB, 0, 0, tiled=True)
    near, far = gradients(every, logits, taught, chosen)

    def passed(value, by):
        return lax.ppermute(value, "x", shift(NX, by))

    near = [near, passed(near, -1), None, passed(near, 1)]
    far = [far, passed(far, -1), None, passed(far, 1)]
    near[2], far[2] = passed(near[1], -1), passed(far[3], 1)

    def rows_of(parts, which):
        return jnp.stack(
            [
                lax.dot_general(
                    parts[r], head, (((0,), (0,)), ((), ())), preferred_element_type=jnp.float32
                )
                for r in which
            ]
        ).reshape(len(which), NY, NZ * OWN, COLS)

    def across(which):
        away = lax.ppermute(rows_of(far, which).astype(jnp.bfloat16), "c", shift(NC, 1))
        both = rows_of(near, which) + away.astype(jnp.float32)
        return both[:, 0], [both[:, by].astype(jnp.bfloat16) for by in range(1, NY)]

    def along(others):
        return [lax.ppermute(part, "y", shift(NY, -by)) for by, part in enumerate(others, 1)]

    def shared(mine, others):
        return (mine + sum(part.astype(jnp.float32) for part in others)).astype(jnp.bfloat16)

    first, others = across((0,))
    first_others = along(others)
    first, near[1], near[3], far[1], far[3] = lax.optimization_barrier(
        (first, near[1], near[3], far[1], far[3])
    )
    first_others, near[2], far[2] = lax.optimization_barrier((first_others, near[2], far[2]))
    rest, others = across((1, 2, 3))
    rest = shared(rest, along(others))
    mine = jnp.concatenate([shared(first, first_others), rest], axis=0)
    mine = rolled(mine, back)
    got = lax.all_to_all(mine.reshape(NX * NZ, OWN, COLS), ("x", "z"), 0, 0, tiled=True)
    total = jnp.sum(got.reshape(NX, NZ, OWN, COLS).astype(jnp.float32), axis=1)
    grad_hidden = total.transpose(1, 0, 2).reshape(OWN, NX * COLS).astype(jnp.bfloat16)
    pieces = [part for pair in zip(near, far) for part in pair]
    grad_head = head_gradient(pieces, rows.reshape(NX * SPAN, COLS))
    return grad_hidden, grad_head.T


def solution(mesh):
    fine = Mesh(mesh.devices.reshape(NX, NZ, NY, NC), ("x", "z", "y", "c"))
    every = ("x", "z", "y", "c")
    placed = (P(every, None), P(every, None), P("x", VOCAB), P(every))
    return jax.shard_map(
        body,
        mesh=fine,
        in_specs=placed,
        out_specs=(P(every, None), P("x", VOCAB)),
        check_vma=False,
    )
```

```python
import jax
import jax.numpy as jnp
from jax import lax
from jax.experimental import pallas as pl
from jax.experimental.pallas import tpu as pltpu
from jax.sharding import Mesh, PartitionSpec as P

alpha_power = 0.5
beta_power = 0.25
joint_power = 0.75
smallest = 1e-37
far_below = -1e30

NX, NZ, NY, NC = 4, 8, 4, 2
VOCAB = ("z", "y", "c")
OWN = 4
COLS = 1280
SLICE = 1187
PADDED = 1200
TILE = 240
CHUNK = 240
LONG = 600
SPAN = 256
HALF = 128


def shift(count, by):
    return [(i, (i + by) % count) for i in range(count)]


def rolled(value, by):
    count = value.shape[0]
    return lax.dynamic_slice_in_dim(jnp.concatenate([value, value], axis=0), by, count, axis=0)


def gather_hidden(hidden, x, *ready):
    pieces = hidden.reshape(OWN, NX, COLS).transpose(1, 0, 2)
    spread = jnp.broadcast_to(pieces[:, None], (NX, NZ, OWN, COLS)).reshape(NX * NZ, OWN, COLS)
    got = lax.all_to_all(spread, ("x", "z"), 0, 0, tiled=True)
    mine = rolled(got.reshape(NX, NZ * OWN, COLS), x)
    mine, *ready = lax.optimization_barrier((mine, *ready))
    near = [mine] + [lax.ppermute(mine, "y", shift(NY, by)) for by in range(1, NY)]
    far = [lax.ppermute(block, "c", shift(NC, 1)) for block in near]
    return near + far, *ready


def order(y, c):
    place = jnp.arange(SPAN)
    core, back, z, own = place // 128, place // 32 % NY, place // OWN % NZ, place % OWN
    true = ((z * NY + (y - back) % NY) * NC + (c + core) % NC) * OWN + own
    return place[:, None] == true[None, :]


def split_three(value):
    high = value.astype(jnp.bfloat16)
    rest = value - high.astype(jnp.float32)
    middle = rest.astype(jnp.bfloat16)
    low = (rest - middle.astype(jnp.float32)).astype(jnp.bfloat16)
    return jnp.stack([high, middle, low], axis=-1)


def teacher_rows(teacher, loss_weight):
    parts = teacher.reshape(OWN, NZ * NY * NC, SLICE)
    weights = jnp.pad(split_three(loss_weight), ((0, 0), (0, PADDED - SLICE - 3)))
    weights = jnp.broadcast_to(weights[:, None], (OWN, NZ * NY * NC, PADDED - SLICE))
    return jnp.concatenate([parts, weights], axis=2).transpose(1, 0, 2)


def gather_teacher(rows, chosen):
    got = lax.all_to_all(rows, VOCAB, 0, 0, tiled=True).reshape(SPAN, PADDED)
    return lax.dot_general(
        got,
        chosen.astype(jnp.bfloat16),
        (((0,), (0,)), ((), ())),
        preferred_element_type=jnp.float32,
    )


def code(value):
    square = value * value
    fourth = square * square
    return (fourth * fourth * value).astype(jnp.bfloat16)


def decode(coded):
    value = coded.astype(jnp.float32)
    size = jnp.abs(value)
    root = jnp.exp2(jnp.log2(jnp.maximum(size, 1e-37)) * (1.0 / 9.0))
    return jnp.where(value < 0.0, -root, jnp.where(value > 0.0, root, 0.0))


def times(left, right):
    return lax.dot_general(
        left, right, (((1,), (1,)), ((), ())), preferred_element_type=jnp.float32
    )


def local(kernel, outs, scratch, flops, *args):
    place = pl.BlockSpec(memory_space=pltpu.VMEM)
    return pl.pallas_call(
        kernel,
        in_specs=[place] * len(args),
        out_specs=[place] * len(outs),
        out_shape=[jax.ShapeDtypeStruct(shape, dtype) for shape, dtype in outs],
        scratch_shapes=scratch,
        cost_estimate=pl.CostEstimate(flops=flops, bytes_accessed=10**6, transcendentals=0),
        compiler_params=pltpu.CompilerParams(vmem_limit_bytes=12 * 2**20),
    )(*args)


def whole(shape):
    return pl.BlockSpec(shape, lambda *_: (0,) * len(shape))


def streamed(kernel, outs, flops, *args):
    return pl.pallas_call(
        kernel,
        grid=(1,),
        in_specs=[whole(arg.shape) for arg in args],
        out_specs=[whole(shape) for shape, _ in outs],
        out_shape=[jax.ShapeDtypeStruct(shape, dtype) for shape, dtype in outs],
        cost_estimate=pl.CostEstimate(flops=flops, bytes_accessed=5 * 10**6, transcendentals=0),
        compiler_params=pltpu.CompilerParams(vmem_limit_bytes=40 * 2**20),
    )(*args)


PIECE = ((PADDED, HALF), jnp.bfloat16)
KEPT = ((PADDED, HALF), jnp.float32)


def chunks(size, step, start):
    def at(i, carry):
        return step(pl.ds(pl.multiple_of(i * size, size), size), i, carry)

    return lax.fori_loop(0, PADDED // size, at, start)


def relayed_partials(head, blocks):
    def kernel(head_ref, *refs):
        refs, (near_ref, far_ref, rows_ref) = refs[:8], refs[8:]
        for at, ref in enumerate(refs):
            rows_ref[32 * at : 32 * at + 32] = ref[2]

        got = times(head_ref[...], rows_ref[...])
        near_ref[...] = code(got[:, :HALF])
        far_ref[...] = code(got[:, HALF:])

    return local(
        kernel,
        [PIECE, PIECE],
        [pltpu.VMEM((SPAN, COLS), jnp.bfloat16)],
        2 * PADDED * SPAN * COLS,
        head,
        *blocks,
    )


def other_partials(head, blocks):
    def kernel(head_ref, *refs):
        refs, (out_ref, near3_ref, far1_ref, near1_ref, far3_ref, own_ref, rows_ref, done) = (
            refs[:8],
            refs[8:],
        )
        for at, ref in enumerate(refs):
            rows_ref[:, 32 * at : 32 * at + 32] = ref[...]
        copy = pltpu.make_async_copy(rows_ref, out_ref, done)
        copy.start()

        def step(rows, i, carry):
            left = head_ref[rows, :]
            got = times(left, rows_ref[3])
            near3_ref[rows, :] = code(got[:, :HALF])
            far3_ref[rows, :] = got[:, HALF:]
            got = times(left, rows_ref[1])
            near1_ref[rows, :] = got[:, :HALF]
            far1_ref[rows, :] = code(got[:, HALF:])
            own_ref[rows, :] = times(left, rows_ref[0])
            return carry

        chunks(LONG, step, 0)
        copy.wait()

    place = pl.BlockSpec(memory_space=pltpu.VMEM)
    every = ((NX, SPAN, COLS), jnp.bfloat16)
    outs = [every, PIECE, PIECE, KEPT, KEPT, ((PADDED, SPAN), jnp.float32)]
    return pl.pallas_call(
        kernel,
        in_specs=[place] * 9,
        out_specs=[pl.BlockSpec(memory_space=pl.ANY)] + [place] * 5,
        out_shape=[jax.ShapeDtypeStruct(shape, dtype) for shape, dtype in outs],
        scratch_shapes=[pltpu.VMEM(*every), pltpu.SemaphoreType.DMA],
        cost_estimate=pl.CostEstimate(
            flops=6 * PADDED * SPAN * COLS, bytes_accessed=4 * 10**6, transcendentals=0
        ),
        compiler_params=pltpu.CompilerParams(vmem_limit_bytes=16 * 2**20),
    )(head, *blocks)


def added(kept, arrived):
    def kernel(*refs):
        def step(rows, i, carry):
            for ours, theirs, out in zip(refs[:2], refs[2:4], refs[4:]):
                out[rows, :] = code(ours[rows, :] + decode(theirs[rows, :]))
            return carry

        chunks(CHUNK, step, 0)

    return local(kernel, [PIECE, PIECE], [], 40 * PADDED * SPAN, *kept, *arrived)


def valid(i):
    return lax.broadcasted_iota(jnp.int32, (CHUNK, SPAN), 0) + i * CHUNK < SLICE


def folded(value, join):
    return join(value.reshape(CHUNK // 8, 8, SPAN), axis=0)


def exact(left, right, dims):
    return lax.dot_general(
        left, right, (dims, ((), ())), precision=lax.Precision.HIGHEST, preferred_element_type=jnp.float32
    )


def prepared(own, parts, teacher):
    def kernel(own_ref, near_ref, far_ref, teacher_ref, base_ref, rows_ref):
        def first(rows, i, top):
            arrived = jnp.concatenate([decode(near_ref[rows, :]), decode(far_ref[rows, :])], axis=1)
            base_ref[rows, :] = own_ref[rows, :] + arrived
            taught = jnp.where(valid(i), teacher_ref[rows, :], far_below)
            return jnp.maximum(top, folded(taught, jnp.max))

        top = chunks(CHUNK, first, jnp.full((8, SPAN), far_below, jnp.float32))
        top = jnp.max(top, axis=0, keepdims=True)

        def second(rows, i, total):
            taught = jnp.where(valid(i), teacher_ref[rows, :] - top, far_below)
            return total + folded(jnp.exp(taught), jnp.sum)

        total = chunks(CHUNK, second, jnp.zeros((8, SPAN), jnp.float32))
        whole_sum = top + jnp.log(jnp.sum(total, axis=0, keepdims=True))
        rows_ref[...] = jnp.concatenate([top] * 4 + [whole_sum] * 4, axis=0)

    return streamed(
        kernel,
        [((PADDED, SPAN), jnp.float32), ((8, SPAN), jnp.float32)],
        40 * PADDED * SPAN,
        own,
        *parts,
        teacher,
    )


def statistics(base, parts, teacher, taught_rows, chosen):
    def kernel(base_ref, near_ref, far_ref, teacher_ref, taught_ref, chosen_ref, logits_ref, sums_ref):
        def first(rows, i, top):
            arrived = jnp.concatenate([decode(near_ref[rows, :]), decode(far_ref[rows, :])], axis=1)
            student = jnp.where(valid(i), base_ref[rows, :] + arrived, far_below)
            logits_ref[rows, :] = student
            return jnp.maximum(top, folded(student, jnp.max))

        top_s = chunks(CHUNK, first, jnp.full((8, SPAN), far_below, jnp.float32))
        top_s = jnp.max(top_s, axis=0, keepdims=True)
        top_t = taught_ref[0:1, :]

        def second(rows, i, sums):
            s = logits_ref[rows, :] - top_s
            t = jnp.where(valid(i), teacher_ref[rows, :] - top_t, far_below)
            terms = (s, alpha_power * t + beta_power * s, joint_power * s)
            return tuple(so_far + folded(jnp.exp(term), jnp.sum) for so_far, term in zip(sums, terms))

        sums = chunks(CHUNK, second, (jnp.zeros((8, SPAN), jnp.float32),) * 3)
        tops = (top_s, alpha_power * top_t + beta_power * top_s, joint_power * top_s)
        rows = [
            top + jnp.log(jnp.maximum(jnp.sum(total, axis=0, keepdims=True), smallest))
            for top, total in zip(tops, sums)
        ]
        rows = [rows[0], taught_ref[4:5, :], rows[1], rows[2]]
        rows = exact(jnp.concatenate(rows + rows, axis=0), chosen_ref[...], ((1,), (1,)))
        packed = jnp.concatenate([rows[:4, :HALF], rows[:4, HALF:]], axis=0)
        sums_ref[...] = jnp.broadcast_to(packed[None], sums_ref.shape)

    return streamed(
        kernel,
        [((PADDED, SPAN), jnp.float32), ((NZ * NY * NC, 8, HALF), jnp.float32)],
        100 * PADDED * SPAN,
        base,
        *parts,
        teacher,
        taught_rows,
        chosen,
    )


def gradients(every, logits, teacher, chosen):
    def kernel(every_ref, logits_ref, teacher_ref, chosen_ref, near_ref, far_ref):
        sums = every_ref[...]
        top = jnp.max(sums, axis=0)
        merged = top + jnp.log(jnp.sum(jnp.exp(sums - top[None]), axis=0))
        merged = jnp.concatenate([merged[:4], merged[4:]], axis=1)
        merged = exact(jnp.concatenate([merged, merged], axis=0), chosen_ref[...], ((1,), (0,)))
        log_s, log_t, log_m, log_j = (merged[k : k + 1] for k in range(4))
        remainder = jnp.exp(log_m - alpha_power * log_t - beta_power * log_s) - jnp.exp(
            log_j - joint_power * log_s
        )
        tail = teacher_ref[SLICE - 3 : SLICE + 5, :]
        weight = -(tail[3:4] + tail[4:5] + tail[5:6]) / alpha_power

        def step(rows, i, carry):
            s = logits_ref[rows, :] - log_s
            t = jnp.where(valid(i), teacher_ref[rows, :] - log_t, far_below)
            got = (
                jnp.exp(alpha_power * t + beta_power * s)
                - jnp.exp(joint_power * s)
                - jnp.exp(s) * remainder
            )
            got = (weight * got).astype(jnp.bfloat16)
            near_ref[rows, :] = got[:, :HALF]
            far_ref[rows, :] = got[:, HALF:]
            return carry

        chunks(CHUNK, step, 0)

    return streamed(
        kernel, [PIECE, PIECE], 60 * PADDED * SPAN, every, logits, teacher, chosen
    )


def head_gradient(pieces, rows):
    def kernel(*refs):
        left = jnp.concatenate([ref[...] for ref in refs[:8]], axis=1)
        refs[9][...] = jnp.dot(left, refs[8][...], preferred_element_type=jnp.float32).astype(
            jnp.bfloat16
        )

    def tiled(width):
        return pl.BlockSpec((TILE, width), lambda i: (i, 0))

    return pl.pallas_call(
        kernel,
        grid=(PADDED // TILE,),
        in_specs=[tiled(HALF)] * 8 + [pl.BlockSpec((NX * SPAN, COLS), lambda i: (0, 0))],
        out_specs=tiled(COLS),
        out_shape=jax.ShapeDtypeStruct((SLICE, COLS), jnp.bfloat16),
        cost_estimate=pl.CostEstimate(
            flops=2 * PADDED * COLS * NX * SPAN, bytes_accessed=9 * 10**6, transcendentals=0
        ),
        compiler_params=pltpu.CompilerParams(vmem_limit_bytes=20 * 2**20),
    )(*pieces, rows)


def body(hidden, teacher, head_weight, loss_weight):
    x, y, c = lax.axis_index("x"), lax.axis_index("y"), lax.axis_index("c")
    head = jnp.pad(head_weight.T, ((0, PADDED - SLICE), (0, 0)))
    chosen = order(y, c).astype(jnp.float32)
    back = lax.rem(NX - x, NX).astype(jnp.uint32)
    blocks, taught, head, back = gather_hidden(
        hidden, x, teacher_rows(teacher, loss_weight), head, back
    )

    def sent(value, by):
        return lax.ppermute(value, "x", shift(NX, by))

    relay = relayed_partials(head, blocks)
    relay = [sent(relay[0], 1), sent(relay[1], -1)]
    rows, near3, far1, near1, far3, own = other_partials(head, blocks)
    direct = [sent(near3, -1), sent(far1, 1)]
    summed = added((near1, far3), relay)
    summed = [sent(summed[0], 1), sent(summed[1], -1)]
    taught = gather_teacher(taught, chosen)
    base, taught_rows = prepared(own, direct, taught)
    logits, sums = statistics(base, summed, taught, taught_rows, chosen)
    every = lax.all_to_all(sums, VOCAB, 0, 0, tiled=True)
    near, far = gradients(every, logits, taught, chosen)

    def passed(value, by):
        return lax.ppermute(value, "x", shift(NX, by))

    near = [near, passed(near, -1), None, passed(near, 1)]
    far = [far, passed(far, -1), None, passed(far, 1)]
    near[2], far[2] = passed(near[1], -1), passed(far[3], 1)

    def rows_of(parts, which):
        return jnp.stack(
            [
                lax.dot_general(
                    parts[r], head, (((0,), (0,)), ((), ())), preferred_element_type=jnp.float32
                )
                for r in which
            ]
        ).reshape(len(which), NY, NZ * OWN, COLS)

    def across(which):
        away = lax.ppermute(rows_of(far, which).astype(jnp.bfloat16), "c", shift(NC, 1))
        both = rows_of(near, which) + away.astype(jnp.float32)
        return both[:, 0], [both[:, by].astype(jnp.bfloat16) for by in range(1, NY)]

    def along(others):
        return [lax.ppermute(part, "y", shift(NY, -by)) for by, part in enumerate(others, 1)]

    def shared(mine, others):
        return (mine + sum(part.astype(jnp.float32) for part in others)).astype(jnp.bfloat16)

    first, others = across((0,))
    first_others = along(others)
    first, near[1], near[3], far[1], far[3] = lax.optimization_barrier(
        (first, near[1], near[3], far[1], far[3])
    )
    first_others, near[2], far[2] = lax.optimization_barrier((first_others, near[2], far[2]))
    rest, others = across((1, 2, 3))
    rest = shared(rest, along(others))
    mine = jnp.concatenate([shared(first, first_others), rest], axis=0)
    mine = rolled(mine, back)
    got = lax.all_to_all(mine.reshape(NX * NZ, OWN, COLS), ("x", "z"), 0, 0, tiled=True)
    total = jnp.sum(got.reshape(NX, NZ, OWN, COLS).astype(jnp.float32), axis=1)
    grad_hidden = total.transpose(1, 0, 2).reshape(OWN, NX * COLS).astype(jnp.bfloat16)
    pieces = [part for pair in zip(near, far) for part in pair]
    grad_head = head_gradient(pieces, rows.reshape(NX * SPAN, COLS))
    return grad_hidden, grad_head.T


def solution(mesh):
    fine = Mesh(mesh.devices.reshape(NX, NZ, NY, NC), ("x", "z", "y", "c"))
    every = ("x", "z", "y", "c")
    placed = (P(every, None), P(every, None), P("x", VOCAB), P(every))
    return jax.shard_map(
        body,
        mesh=fine,
        in_specs=placed,
        out_specs=(P(every, None), P("x", VOCAB)),
        check_vma=False,
    )
```

```python
import jax
import jax.numpy as jnp
from jax import lax
from jax.experimental import pallas as pl
from jax.experimental.pallas import tpu as pltpu
from jax.sharding import Mesh, PartitionSpec as P

alpha_power = 0.5
beta_power = 0.25
joint_power = 0.75
smallest = 1e-37
far_below = -1e30

NX, NZ, NY, NC = 4, 8, 4, 2
VOCAB = ("z", "y", "c")
OWN = 4
COLS = 1280
SLICE = 1187
PADDED = 1200
TILE = 240
CHUNK = 240
LONG = 600
SPAN = 256
HALF = 128


def shift(count, by):
    return [(i, (i + by) % count) for i in range(count)]


def rolled(value, by):
    count = value.shape[0]
    return lax.dynamic_slice_in_dim(jnp.concatenate([value, value], axis=0), by, count, axis=0)


def gather_hidden(hidden, x, head, *ready):
    pieces = hidden.reshape(OWN, NX, COLS).transpose(1, 0, 2)
    spread = jnp.broadcast_to(pieces[:, None], (NX, NZ, OWN, COLS)).reshape(NX * NZ, OWN, COLS)
    got = lax.all_to_all(spread, ("x", "z"), 0, 0, tiled=True)
    mine = rolled(got.reshape(NX, NZ * OWN, COLS), x)
    mine, *ready = lax.optimization_barrier((mine, *ready))
    near = [mine] + [lax.ppermute(mine, "y", shift(NY, by)) for by in range(1, NY)]
    far = [lax.ppermute(block, "c", shift(NC, 1)) for block in near]
    far[0], head = lax.optimization_barrier((far[0], head))
    return near + far, head, *ready


def order(y, c):
    place = jnp.arange(SPAN)
    core, back, z, own = place // 128, place // 32 % NY, place // OWN % NZ, place % OWN
    true = ((z * NY + (y - back) % NY) * NC + (c + core) % NC) * OWN + own
    return place[:, None] == true[None, :]


def split_three(value):
    high = value.astype(jnp.bfloat16)
    rest = value - high.astype(jnp.float32)
    middle = rest.astype(jnp.bfloat16)
    low = (rest - middle.astype(jnp.float32)).astype(jnp.bfloat16)
    return jnp.stack([high, middle, low], axis=-1)


def teacher_rows(teacher, loss_weight):
    parts = teacher.reshape(OWN, NZ * NY * NC, SLICE)
    weights = jnp.pad(split_three(loss_weight), ((0, 0), (0, PADDED - SLICE - 3)))
    weights = jnp.broadcast_to(weights[:, None], (OWN, NZ * NY * NC, PADDED - SLICE))
    return jnp.concatenate([parts, weights], axis=2).transpose(1, 0, 2)


def gather_teacher(rows, chosen):
    got = lax.all_to_all(rows, VOCAB, 0, 0, tiled=True).reshape(SPAN, PADDED)
    return lax.dot_general(
        got,
        chosen.astype(jnp.bfloat16),
        (((0,), (0,)), ((), ())),
        preferred_element_type=jnp.float32,
    )


def code(value):
    square = value * value
    fourth = square * square
    return (fourth * fourth * value).astype(jnp.bfloat16)


def decode(coded):
    value = coded.astype(jnp.float32)
    size = jnp.abs(value)
    root = jnp.exp2(jnp.log2(jnp.maximum(size, 1e-37)) * (1.0 / 9.0))
    return jnp.where(value < 0.0, -root, jnp.where(value > 0.0, root, 0.0))


def times(left, right):
    return lax.dot_general(
        left, right, (((1,), (1,)), ((), ())), preferred_element_type=jnp.float32
    )


def local(kernel, outs, scratch, flops, *args):
    place = pl.BlockSpec(memory_space=pltpu.VMEM)
    return pl.pallas_call(
        kernel,
        in_specs=[place] * len(args),
        out_specs=[place] * len(outs),
        out_shape=[jax.ShapeDtypeStruct(shape, dtype) for shape, dtype in outs],
        scratch_shapes=scratch,
        cost_estimate=pl.CostEstimate(flops=flops, bytes_accessed=10**6, transcendentals=0),
        compiler_params=pltpu.CompilerParams(vmem_limit_bytes=12 * 2**20),
    )(*args)


def whole(shape):
    return pl.BlockSpec(shape, lambda *_: (0,) * len(shape))


def streamed(kernel, outs, flops, *args):
    return pl.pallas_call(
        kernel,
        grid=(1,),
        in_specs=[whole(arg.shape) for arg in args],
        out_specs=[whole(shape) for shape, _ in outs],
        out_shape=[jax.ShapeDtypeStruct(shape, dtype) for shape, dtype in outs],
        cost_estimate=pl.CostEstimate(flops=flops, bytes_accessed=5 * 10**6, transcendentals=0),
        compiler_params=pltpu.CompilerParams(vmem_limit_bytes=40 * 2**20),
    )(*args)


PIECE = ((PADDED, HALF), jnp.bfloat16)
KEPT = ((PADDED, HALF), jnp.float32)


def chunks(size, step, start):
    def at(i, carry):
        return step(pl.ds(pl.multiple_of(i * size, size), size), i, carry)

    return lax.fori_loop(0, PADDED // size, at, start)


def relayed_partials(head, blocks):
    def kernel(head_ref, *refs):
        refs, (near_ref, far_ref, rows_ref) = refs[:8], refs[8:]
        for at, ref in enumerate(refs):
            rows_ref[32 * at : 32 * at + 32] = ref[2]

        got = times(head_ref[...], rows_ref[...])
        near_ref[...] = code(got[:, :HALF])
        far_ref[...] = code(got[:, HALF:])

    return local(
        kernel,
        [PIECE, PIECE],
        [pltpu.VMEM((SPAN, COLS), jnp.bfloat16)],
        2 * PADDED * SPAN * COLS,
        head,
        *blocks,
    )


def other_partials(head, blocks):
    def kernel(head_ref, *refs):
        refs, (out_ref, near3_ref, far1_ref, near1_ref, far3_ref, own_ref, rows_ref, done) = (
            refs[:8],
            refs[8:],
        )
        for at, ref in enumerate(refs):
            rows_ref[:, 32 * at : 32 * at + 32] = ref[...]
        copy = pltpu.make_async_copy(rows_ref, out_ref, done)
        copy.start()

        def step(rows, i, carry):
            left = head_ref[rows, :]
            got = times(left, rows_ref[3])
            near3_ref[rows, :] = code(got[:, :HALF])
            far3_ref[rows, :] = got[:, HALF:]
            got = times(left, rows_ref[1])
            near1_ref[rows, :] = got[:, :HALF]
            far1_ref[rows, :] = code(got[:, HALF:])
            own_ref[rows, :] = times(left, rows_ref[0])
            return carry

        chunks(LONG, step, 0)
        copy.wait()

    place = pl.BlockSpec(memory_space=pltpu.VMEM)
    every = ((NX, SPAN, COLS), jnp.bfloat16)
    outs = [every, PIECE, PIECE, KEPT, KEPT, ((PADDED, SPAN), jnp.float32)]
    return pl.pallas_call(
        kernel,
        in_specs=[place] * 9,
        out_specs=[pl.BlockSpec(memory_space=pl.ANY)] + [place] * 5,
        out_shape=[jax.ShapeDtypeStruct(shape, dtype) for shape, dtype in outs],
        scratch_shapes=[pltpu.VMEM(*every), pltpu.SemaphoreType.DMA],
        cost_estimate=pl.CostEstimate(
            flops=6 * PADDED * SPAN * COLS, bytes_accessed=4 * 10**6, transcendentals=0
        ),
        compiler_params=pltpu.CompilerParams(vmem_limit_bytes=16 * 2**20),
    )(head, *blocks)


def added(kept, arrived):
    def kernel(*refs):
        def step(rows, i, carry):
            for ours, theirs, out in zip(refs[:2], refs[2:4], refs[4:]):
                out[rows, :] = code(ours[rows, :] + decode(theirs[rows, :]))
            return carry

        chunks(CHUNK, step, 0)

    return local(kernel, [PIECE, PIECE], [], 40 * PADDED * SPAN, *kept, *arrived)


def valid(i):
    return lax.broadcasted_iota(jnp.int32, (CHUNK, SPAN), 0) + i * CHUNK < SLICE


def folded(value, join):
    return join(value.reshape(CHUNK // 8, 8, SPAN), axis=0)


def exact(left, right, dims):
    return lax.dot_general(
        left, right, (dims, ((), ())), precision=lax.Precision.HIGHEST, preferred_element_type=jnp.float32
    )


def prepared(own, parts, teacher):
    def kernel(own_ref, near_ref, far_ref, teacher_ref, base_ref, rows_ref):
        def first(rows, i, top):
            arrived = jnp.concatenate([decode(near_ref[rows, :]), decode(far_ref[rows, :])], axis=1)
            base_ref[rows, :] = own_ref[rows, :] + arrived
            taught = jnp.where(valid(i), teacher_ref[rows, :], far_below)
            return jnp.maximum(top, folded(taught, jnp.max))

        top = chunks(CHUNK, first, jnp.full((8, SPAN), far_below, jnp.float32))
        top = jnp.max(top, axis=0, keepdims=True)

        def second(rows, i, total):
            taught = jnp.where(valid(i), teacher_ref[rows, :] - top, far_below)
            return total + folded(jnp.exp(taught), jnp.sum)

        total = chunks(CHUNK, second, jnp.zeros((8, SPAN), jnp.float32))
        whole_sum = top + jnp.log(jnp.sum(total, axis=0, keepdims=True))
        rows_ref[...] = jnp.concatenate([top] * 4 + [whole_sum] * 4, axis=0)

    return streamed(
        kernel,
        [((PADDED, SPAN), jnp.float32), ((8, SPAN), jnp.float32)],
        40 * PADDED * SPAN,
        own,
        *parts,
        teacher,
    )


def statistics(base, parts, teacher, taught_rows, chosen):
    def kernel(base_ref, near_ref, far_ref, teacher_ref, taught_ref, chosen_ref, logits_ref, sums_ref):
        def first(rows, i, top):
            arrived = jnp.concatenate([decode(near_ref[rows, :]), decode(far_ref[rows, :])], axis=1)
            student = jnp.where(valid(i), base_ref[rows, :] + arrived, far_below)
            logits_ref[rows, :] = student
            return jnp.maximum(top, folded(student, jnp.max))

        top_s = chunks(CHUNK, first, jnp.full((8, SPAN), far_below, jnp.float32))
        top_s = jnp.max(top_s, axis=0, keepdims=True)
        top_t = taught_ref[0:1, :]

        def second(rows, i, sums):
            s = logits_ref[rows, :] - top_s
            t = jnp.where(valid(i), teacher_ref[rows, :] - top_t, far_below)
            terms = (s, alpha_power * t + beta_power * s, joint_power * s)
            return tuple(so_far + folded(jnp.exp(term), jnp.sum) for so_far, term in zip(sums, terms))

        sums = chunks(CHUNK, second, (jnp.zeros((8, SPAN), jnp.float32),) * 3)
        tops = (top_s, alpha_power * top_t + beta_power * top_s, joint_power * top_s)
        rows = [
            top + jnp.log(jnp.maximum(jnp.sum(total, axis=0, keepdims=True), smallest))
            for top, total in zip(tops, sums)
        ]
        rows = [rows[0], taught_ref[4:5, :], rows[1], rows[2]]
        rows = exact(jnp.concatenate(rows + rows, axis=0), chosen_ref[...], ((1,), (1,)))
        packed = jnp.concatenate([rows[:4, :HALF], rows[:4, HALF:]], axis=0)
        sums_ref[...] = jnp.broadcast_to(packed[None], sums_ref.shape)

    return streamed(
        kernel,
        [((PADDED, SPAN), jnp.float32), ((NZ * NY * NC, 8, HALF), jnp.float32)],
        100 * PADDED * SPAN,
        base,
        *parts,
        teacher,
        taught_rows,
        chosen,
    )


def gradients(every, logits, teacher, chosen):
    def kernel(every_ref, logits_ref, teacher_ref, chosen_ref, near_ref, far_ref):
        sums = every_ref[...]
        top = jnp.max(sums, axis=0)
        merged = top + jnp.log(jnp.sum(jnp.exp(sums - top[None]), axis=0))
        merged = jnp.concatenate([merged[:4], merged[4:]], axis=1)
        merged = exact(jnp.concatenate([merged, merged], axis=0), chosen_ref[...], ((1,), (0,)))
        log_s, log_t, log_m, log_j = (merged[k : k + 1] for k in range(4))
        remainder = jnp.exp(log_m - alpha_power * log_t - beta_power * log_s) - jnp.exp(
            log_j - joint_power * log_s
        )
        tail = teacher_ref[SLICE - 3 : SLICE + 5, :]
        weight = -(tail[3:4] + tail[4:5] + tail[5:6]) / alpha_power

        def step(rows, i, carry):
            s = logits_ref[rows, :] - log_s
            t = jnp.where(valid(i), teacher_ref[rows, :] - log_t, far_below)
            got = (
                jnp.exp(alpha_power * t + beta_power * s)
                - jnp.exp(joint_power * s)
                - jnp.exp(s) * remainder
            )
            got = (weight * got).astype(jnp.bfloat16)
            near_ref[rows, :] = got[:, :HALF]
            far_ref[rows, :] = got[:, HALF:]
            return carry

        chunks(CHUNK, step, 0)

    return streamed(
        kernel, [PIECE, PIECE], 60 * PADDED * SPAN, every, logits, teacher, chosen
    )


def head_gradient(pieces, rows):
    def kernel(*refs):
        left = jnp.concatenate([ref[...] for ref in refs[:8]], axis=1)
        refs[9][...] = jnp.dot(left, refs[8][...], preferred_element_type=jnp.float32).astype(
            jnp.bfloat16
        )

    def tiled(width):
        return pl.BlockSpec((TILE, width), lambda i: (i, 0))

    return pl.pallas_call(
        kernel,
        grid=(PADDED // TILE,),
        in_specs=[tiled(HALF)] * 8 + [pl.BlockSpec((NX * SPAN, COLS), lambda i: (0, 0))],
        out_specs=tiled(COLS),
        out_shape=jax.ShapeDtypeStruct((SLICE, COLS), jnp.bfloat16),
        cost_estimate=pl.CostEstimate(
            flops=2 * PADDED * COLS * NX * SPAN, bytes_accessed=9 * 10**6, transcendentals=0
        ),
        compiler_params=pltpu.CompilerParams(vmem_limit_bytes=20 * 2**20),
    )(*pieces, rows)


def body(hidden, teacher, head_weight, loss_weight):
    x, y, c = lax.axis_index("x"), lax.axis_index("y"), lax.axis_index("c")
    head = jnp.pad(head_weight.T, ((0, PADDED - SLICE), (0, 0)))
    chosen = order(y, c).astype(jnp.float32)
    back = lax.rem(NX - x, NX).astype(jnp.uint32)
    blocks, head, taught, back = gather_hidden(
        hidden, x, head, teacher_rows(teacher, loss_weight), back
    )

    def sent(value, by):
        return lax.ppermute(value, "x", shift(NX, by))

    relay = relayed_partials(head, blocks)
    relay = [sent(relay[0], 1), sent(relay[1], -1)]
    rows, near3, far1, near1, far3, own = other_partials(head, blocks)
    direct = [sent(near3, -1), sent(far1, 1)]
    summed = added((near1, far3), relay)
    summed = [sent(summed[0], 1), sent(summed[1], -1)]
    taught = gather_teacher(taught, chosen)
    base, taught_rows = prepared(own, direct, taught)
    logits, sums = statistics(base, summed, taught, taught_rows, chosen)
    every = lax.all_to_all(sums, VOCAB, 0, 0, tiled=True)
    near, far = gradients(every, logits, taught, chosen)

    def passed(value, by):
        return lax.ppermute(value, "x", shift(NX, by))

    near = [near, passed(near, -1), None, passed(near, 1)]
    far = [far, passed(far, -1), None, passed(far, 1)]
    near[2], far[2] = passed(near[1], -1), passed(far[3], 1)

    def rows_of(parts, which):
        return jnp.stack(
            [
                lax.dot_general(
                    parts[r], head, (((0,), (0,)), ((), ())), preferred_element_type=jnp.float32
                )
                for r in which
            ]
        ).reshape(len(which), NY, NZ * OWN, COLS)

    def across(which):
        away = lax.ppermute(rows_of(far, which).astype(jnp.bfloat16), "c", shift(NC, 1))
        both = rows_of(near, which) + away.astype(jnp.float32)
        return both[:, 0], [both[:, by].astype(jnp.bfloat16) for by in range(1, NY)]

    def along(others):
        return [lax.ppermute(part, "y", shift(NY, -by)) for by, part in enumerate(others, 1)]

    def shared(mine, others):
        return (mine + sum(part.astype(jnp.float32) for part in others)).astype(jnp.bfloat16)

    first, others = across((0,))
    first_others = along(others)
    first, near[1], near[3], far[1], far[3] = lax.optimization_barrier(
        (first, near[1], near[3], far[1], far[3])
    )
    first_others, near[2], far[2] = lax.optimization_barrier((first_others, near[2], far[2]))
    rest, others = across((1, 2, 3))
    rest = shared(rest, along(others))
    mine = jnp.concatenate([shared(first, first_others), rest], axis=0)
    mine = rolled(mine, back)
    got = lax.all_to_all(mine.reshape(NX * NZ, OWN, COLS), ("x", "z"), 0, 0, tiled=True)
    total = jnp.sum(got.reshape(NX, NZ, OWN, COLS).astype(jnp.float32), axis=1)
    grad_hidden = total.transpose(1, 0, 2).reshape(OWN, NX * COLS).astype(jnp.bfloat16)
    pieces = [part for pair in zip(near, far) for part in pair]
    grad_head = head_gradient(pieces, rows.reshape(NX * SPAN, COLS))
    return grad_hidden, grad_head.T


def solution(mesh):
    fine = Mesh(mesh.devices.reshape(NX, NZ, NY, NC), ("x", "z", "y", "c"))
    every = ("x", "z", "y", "c")
    placed = (P(every, None), P(every, None), P("x", VOCAB), P(every))
    return jax.shard_map(
        body,
        mesh=fine,
        in_specs=placed,
        out_specs=(P(every, None), P("x", VOCAB)),
        check_vma=False,
    )
```
